32 devices in a mesh: dp: 8 (over y, x, core), expert: 4 (over z).
Axes of the slice: x: 2, y: 2, z: 4, core: 2. Of those that a mesh axis runs over, the one named last changes fastest.
Arguments:
- cotangent: bfloat16 [8192, 2048], P(('dp', 'expert')), may hold values from -0.625 to 0.625
- route_weight: float32 [8192], P(('dp', 'expert')), may hold values from 0.1 to 1
- expert_ids: int32 [8192], P(('dp', 'expert')), may hold values from 0 to 3, as said below
- slot_ids: int32 [8192], P(('dp', 'expert')), may hold values from 0 to 127
- hidden_saved: bfloat16 [8, 4, 4, 128, 768], P('dp', 'expert'), may hold values from -6 to 6
- down_weight: float32 [4, 2048, 768], P('expert', 'dp')
- first_moment: float32 [4, 2048, 768], P('expert', 'dp'), may hold values from -3 to 3
- second_moment: float32 [4, 2048, 768], P('expert', 'dp'), may hold values from 0.003 to 0.03
Outputs:
- new_weight: float32 [4, 2048, 768], P('expert', 'dp')
- new_first: float32 [4, 2048, 768], P('expert', 'dp')
- new_second: float32 [4, 2048, 768], P('expert', 'dp')
The draws below stay inside these ranges and needn't reach their ends.
Inputs may be any that keep to these rules, and one draw needn't show every extreme that they name: `expert_ids`: within the rows of one device no pair (expert, slot) repeats, so no expert gets more than 128 rows from one device; in every data group one expert gets exactly 128 rows from each device of the group.
All inputs are finite; a program needn't handle non-finite values.
Results may differ from the reference program's by a relative error of at most 0.00049.
Values may be sent and summed in bfloat16 or wider, within the bound.
No kernel may reach another device: no remote copies, remote signals or barrier semaphores. Data moves between devices by JAX's collectives and lax.ppermute only.
A program may use at most 64 MiB of HBM per device.

```python
import math
import jax
import jax.numpy as jnp
from jax import lax

D = 2048
FF = 768
TOK_DEV = 256
EXPERTS = 4
CAP = 128
TOKENS = 8192
N_DP = 8


def routing(key):
    blocks = TOKENS // TOK_DEV
    groups = blocks // EXPERTS
    full = jax.random.randint(jax.random.fold_in(key, 1), (groups,), 0, EXPERTS)
    full_block = jnp.repeat(full, EXPERTS)
    keys = jax.random.split(jax.random.fold_in(key, 2), blocks)
    total = EXPERTS * CAP

    def one_block(block_key, favored):
        first_key, second_key = jax.random.split(block_key)
        shuffled = jax.random.permutation(first_key, total)
        owner = shuffled // CAP
        rank = jnp.where(owner == favored, 0, 1) * total + jnp.arange(total)
        chosen = shuffled[jnp.argsort(rank, stable=True)][:TOK_DEV]
        return chosen[jax.random.permutation(second_key, TOK_DEV)]
    chosen = jax.vmap(one_block)(keys, full_block).reshape(-1).astype(jnp.int32)
    return (chosen // CAP, chosen % CAP)


def draw_expert_ids(key, part):
    return routing(key)[0].astype(jnp.int32)


def draw_slot_ids(key, part):
    return routing(key)[1].astype(jnp.int32)


def draw_down_weight(key, part):
    key = jax.random.fold_in(key, 11)
    noise_key, column_key = jax.random.split(key)
    position = jnp.arange(D, dtype=jnp.float32) / max(D - 1, 1)
    noise = jax.random.normal(noise_key, (EXPERTS, D, FF), jnp.float32)
    row_scale = 10.0 ** position
    column_scale = jnp.exp(jax.random.uniform(column_key, (EXPERTS, 1, FF), jnp.float32) * jnp.log(10.0))
    base = 0.04
    return base * noise * row_scale[None, :, None] * column_scale


def with_spikes(drawn, key, source, target, shards_of, factor):
    def block_of(dim):
        return (jnp.arange(drawn.shape[dim]) // (drawn.shape[dim] // shards_of)).reshape((-1,) + (1,) * (drawn.ndim - 1 - dim))

    one_side = jax.random.permutation(key, shards_of)[block_of(target)]
    second = (block_of(target) + shards_of // 2) % shards_of
    return jnp.where((block_of(source) == one_side) | (block_of(source) == second), factor * drawn, drawn)


def level_of(rng, shape, shards, least, top_value):
    level = 1.0
    for axis_at, blocks in shards:
        draws = jax.random.uniform(jax.random.fold_in(jax.random.fold_in(rng, 6), axis_at), (blocks,), jnp.float32, least / len(shards), top_value / len(shards))
        level = level * jnp.repeat(jnp.exp(draws), shape[axis_at] // blocks).reshape((-1,) + (1,) * (len(shape) - 1 - axis_at))
    return level


def normal_values(key, dims, deviation, limit, cuts=(), kind=jnp.bfloat16):
    level = level_of(key, dims, cuts, -0.22, 0.18) if cuts else 1.0
    drawn = jax.random.normal(key, dims, jnp.float32) * deviation * level
    return jnp.minimum(jnp.maximum(drawn, -limit), limit).astype(kind)


def gaussian_with(key, shape, scale, reach, cuts, heavy, kind=jnp.bfloat16):
    drawn = scale * jax.random.normal(key, shape, jnp.float32)
    if cuts:
        drawn = drawn * level_of(key, shape, cuts, -0.22, 0.18)
    return jnp.clip(with_spikes(drawn, jax.random.fold_in(key, 3), *heavy), -reach, reach).astype(kind)


def setup_inputs(seed: int = 0) -> dict:
    splits = jax.random.split(jax.random.key(seed), 9)
    cotangent = gaussian_with(splits[0], (TOKENS, D), ((N_DP * TOK_DEV) ** -0.5), 0.625, ((0, 32),), (0, 1, 32, 2.75))
    route_weight = jnp.clip(jnp.exp(math.log(1.0) - 2.3025851 * jax.random.uniform(splits[1], (TOKENS,), jnp.float32) ** level_of(splits[1], (TOKENS,), ((0, 32),), -0.2, 0.2)), 0.1, 1.0)
    expert_ids = draw_expert_ids(jax.random.fold_in(splits[8], 71), 0)
    slot_ids = draw_slot_ids(jax.random.fold_in(splits[8], 71), 0)
    hidden_saved = normal_values(splits[4], (N_DP, EXPERTS, EXPERTS, CAP, FF), 1.0, 6.0, ((0, 8), (1, 4)))
    down_weight = draw_down_weight(jax.random.fold_in(splits[8], 71), 0)
    first_moment = normal_values(splits[6], (EXPERTS, D, FF), 0.5, 3.0, ((0, 4), (1, 8)), jnp.float32)
    second_moment = jnp.clip(jnp.exp(math.log(0.03) - 2.3025851 * jax.random.uniform(splits[7], (EXPERTS, D, FF), jnp.float32) ** level_of(splits[7], (EXPERTS, D, FF), ((0, 4), (1, 8)), -0.2, 0.2)), 0.003, 0.03)
    return dict(cotangent=cotangent, route_weight=route_weight, expert_ids=expert_ids, slot_ids=slot_ids, hidden_saved=hidden_saved, down_weight=down_weight, first_moment=first_moment, second_moment=second_moment)


def reference(cotangent, route_weight, expert_ids, slot_ids, hidden_saved, down_weight, first_moment, second_moment):
    routed = (route_weight[:, None] * cotangent.astype(jnp.float32)).astype(jnp.bfloat16)
    token = jnp.arange(TOKENS, dtype=jnp.int32)
    block = token // TOK_DEV
    group = block // EXPERTS
    source = block % EXPERTS
    flat = ((group * EXPERTS + expert_ids) * EXPERTS + source) * CAP + slot_ids
    saved_rows = hidden_saved.reshape(-1, FF)[flat]
    order = jnp.argsort(expert_ids, stable=True)
    tile = 2048
    sorted_cot = jnp.concatenate([routed[order], jnp.zeros((tile, D), jnp.bfloat16)], 0)
    sorted_hid = jnp.concatenate([saved_rows[order], jnp.zeros((tile, FF), jnp.bfloat16)], 0)
    labels = jnp.arange(EXPERTS, dtype=jnp.int32)
    counts = lax.optimization_barrier(jnp.sum((expert_ids[None, :] == labels[:, None]).astype(jnp.int32), axis=1))
    starts = jnp.cumsum(counts) - counts

    def per_expert(expert):
        count = counts[expert]
        start = starts[expert]

        def add_tile(step, total):
            begin = (start + step * tile).astype(jnp.int32)
            left = lax.dynamic_slice_in_dim(sorted_cot, begin, tile, 0).astype(jnp.float32)
            right = lax.dynamic_slice_in_dim(sorted_hid, begin, tile, 0).astype(jnp.float32)
            live = (jnp.arange(tile, dtype=jnp.int32) + step * tile < count)[:, None]
            left = jnp.where(live, left, jnp.zeros_like(left))
            return total + lax.dot_general(left, right, (((0,), (0,)), ((), ())), preferred_element_type=jnp.float32)
        steps_needed = (count + tile - 1) // tile
        return lax.fori_loop(jnp.int32(0), steps_needed.astype(jnp.int32), add_tile, jnp.zeros((D, FF), jnp.float32))
    grad = lax.map(per_expert, labels)
    new_first = 0.9 * first_moment + 0.1 * grad
    new_second = 0.999 * second_moment + 0.001 * grad * grad
    update = new_first / (1.0 - 0.9 ** 10) / (jnp.sqrt(new_second / (1.0 - 0.999 ** 10)) + 1e-06) + 0.01 * down_weight
    weight_size = jnp.sqrt(lax.optimization_barrier(jnp.sum(down_weight * down_weight, axis=(1, 2))))
    update_size = jnp.sqrt(lax.optimization_barrier(jnp.sum(update * update, axis=(1, 2))))
    ratio = weight_size / (update_size + 1e-06)
    new_weight = down_weight - 0.1 * ratio[:, None, None] * update
    return (new_weight, new_first, new_second)
```

```python
import functools

import jax
import jax.numpy as jnp
from jax import lax
from jax.experimental import pallas as pl
from jax.experimental.pallas import tpu as pltpu
from jax.sharding import PartitionSpec as P

VMEM = pl.BlockSpec(memory_space=pltpu.VMEM)
TAIL = 16
ROWS_FIRST = (((0,), (0,)), ((), ()))


def on_device(
    cotangent,
    route_weight,
    expert_ids,
    slot_ids,
    hidden_saved,
    down_weight,
    first_moment,
    second_moment,
):
    tok_rows, width = cotangent.shape
    owners = lax.axis_size("expert")
    hidden_rows = hidden_saved.reshape(-1, hidden_saved.shape[-1])
    capacity = hidden_rows.shape[0] // owners
    weight = down_weight[0]
    routed = (route_weight[:, None] * cotangent.astype(jnp.float32)).astype(jnp.bfloat16)
    target = expert_ids * capacity + slot_ids
    outgoing = jnp.zeros((owners * capacity, width), jnp.bfloat16).at[target].set(routed)
    arrived = lax.all_to_all(
        outgoing.reshape(owners, capacity, width), "expert", split_axis=0, concat_axis=0, tiled=True
    )
    arrived = arrived.reshape(owners * capacity, width)
    whole_term = lax.dot_general(
        arrived, hidden_rows, (((0,), (0,)), ((), ())), preferred_element_type=jnp.float32
    )
    grad = lax.psum_scatter(whole_term, "dp", scatter_dimension=0, tiled=True)
    new_first = 0.9 * first_moment[0] + 0.1 * grad
    new_second = 0.999 * second_moment[0] + 0.001 * grad * grad
    update = (
        new_first / (1.0 - 0.9**10) / (jnp.sqrt(new_second / (1.0 - 0.999**10)) + 1e-06)
        + 0.01 * weight
    )
    weight_sq, update_sq = lax.psum((jnp.sum(weight * weight), jnp.sum(update * update)), "dp")
    ratio = jnp.sqrt(weight_sq) / (jnp.sqrt(update_sq) + 1e-06)
    new_weight = weight - 0.1 * ratio * update
    return (new_weight[None], new_first[None], new_second[None])


def cut_kernel(n_dp, cot_ref, scale_ref, expert_ref, slot_ref, *out_refs):
    tokens, width = cot_ref.shape
    part = width // n_dp
    me = lax.axis_index("dp")
    scale = jnp.broadcast_to(scale_ref[...], (128, tokens)).T
    scale = jnp.concatenate([scale] * (part // 128), axis=1)
    row = lax.broadcasted_iota(jnp.int32, (TAIL, tokens), 0)
    ids = jnp.where(row == 0, expert_ref[...], jnp.where(row == 1, slot_ref[...], 0))
    ids = ids.astype(jnp.float32).astype(jnp.bfloat16)
    for mask, out_ref in enumerate(out_refs):
        begin = pl.multiple_of((me ^ mask) * part, part)
        block = cot_ref[:, pl.ds(begin, part)].astype(jnp.float32)
        out_ref[:tokens, :] = (scale * block).astype(jnp.bfloat16)
        out_ref[tokens:, :] = ids


def pack_kernel(owners, capacity, n_blocks, *refs):
    me = lax.axis_index("expert")
    blocks, outs = refs[:n_blocks], refs[n_blocks:]
    tokens = blocks[0].shape[0] - TAIL
    slot = lax.broadcasted_iota(jnp.int32, (capacity, tokens), 0).astype(jnp.float32)
    for at, block in enumerate(blocks):
        ids = block[tokens:, :].astype(jnp.float32)
        place = ids[0:1, :] * capacity + ids[1:2, :]
        rows = block[:tokens, :]
        for shift, out in enumerate(outs):
            expert = lax.rem(me + shift, owners)
            first = (expert * capacity).astype(jnp.float32)
            hot = jnp.where(slot + first == place, 1.0, 0.0).astype(jnp.bfloat16)
            packed = jnp.dot(hot, rows, preferred_element_type=jnp.float32)
            out[at * capacity : (at + 1) * capacity, :] = packed.astype(jnp.bfloat16)


def add_products(owners, capacity, total, packed, hidden):
    me = lax.axis_index("expert")
    for at, parts in enumerate(hidden):
        for shift, rows_ref in enumerate(packed):
            source = lax.rem(me + owners - shift, owners)
            begin = pl.multiple_of(source * capacity, capacity)
            rows = rows_ref[at * capacity : (at + 1) * capacity, :]
            column = 0
            for part in parts:
                wide = part.shape[1]
                total[:, column : column + wide] += lax.dot_general(
                    rows, part[pl.ds(begin, capacity), :], ROWS_FIRST, preferred_element_type=jnp.float32
                )
                column += wide


def split_refs(refs, owners, chunks):
    out, at = [], 0
    for parts in chunks:
        packed = refs[at : at + owners]
        at += owners
        hidden = []
        for n in parts:
            hidden.append(refs[at : at + n])
            at += n
        out.append((packed, hidden))
    return out, refs[at:]


def early_kernel(owners, capacity, chunks, *refs):
    pairs, (total,) = split_refs(refs, owners, chunks)
    total[...] = jnp.zeros_like(total)
    for packed, hidden in pairs:
        add_products(owners, capacity, total, packed, hidden)


def update_kernel(owners, capacity, chunks, *refs):
    pairs, rest = split_refs(refs, owners, chunks)
    early, weight_ref, first_ref, second_ref, new_first, new_second, update_ref, sums, total = rest
    total[...] = early[...]
    for packed, hidden in pairs:
        add_products(owners, capacity, total, packed, hidden)
    grad = total[...]
    weight = weight_ref[0]
    first = 0.9 * first_ref[0] + 0.1 * grad
    second = 0.999 * second_ref[0] + 0.001 * grad * grad
    new_first[0] = first
    new_second[0] = second
    update = first / (1.0 - 0.9**10) / (jnp.sqrt(second / (1.0 - 0.999**10)) + 1e-06) + 0.01 * weight
    update_ref[...] = update
    row = lax.broadcasted_iota(jnp.int32, sums.shape, 0)
    sums[...] = jnp.where(row == 0, jnp.sum(weight * weight), jnp.sum(update * update))


def weight_kernel(n_sums, *refs):
    sums, (weight_ref, update_ref, new_weight) = refs[:n_sums], refs[n_sums:]
    total = sums[0][...]
    for other in sums[1:]:
        total = total + other[...]
    norm = jnp.sqrt(total)
    ratio = norm[0:1, 0:1] / (norm[1:2, 0:1] + 1e-06)
    new_weight[0] = weight_ref[0] - (0.1 * ratio) * update_ref[...]


def call(kernel, out_shape, *args, scratch=(), flops=0, name=None):
    nbytes = sum(a.size * a.dtype.itemsize for a in jax.tree.leaves((args, out_shape)))
    return pl.pallas_call(
        kernel,
        out_shape=out_shape,
        in_specs=[VMEM] * len(args),
        out_specs=jax.tree.map(lambda _: VMEM, out_shape),
        scratch_shapes=scratch,
        compiler_params=pltpu.CompilerParams(vmem_limit_bytes=40 * 2**20),
        cost_estimate=pl.CostEstimate(flops=flops, bytes_accessed=nbytes, transcendentals=0),
        name=name,
    )(*args)


def by_permutes(
    cotangent,
    route_weight,
    expert_ids,
    slot_ids,
    hidden_saved,
    down_weight,
    first_moment,
    second_moment,
):
    n_dp, owners = lax.axis_size("dp"), lax.axis_size("expert")
    tokens, width = cotangent.shape
    capacity, ff = hidden_saved.shape[3:]
    part = width // n_dp
    bf16, f32 = jnp.bfloat16, jnp.float32
    hidden = hidden_saved.reshape(owners * capacity, ff)

    def across(array, mask):
        return lax.ppermute(array, "dp", [(d, d ^ mask) for d in range(n_dp)])

    def along(array, shift):
        return lax.ppermute(array, "expert", [(d, (d + shift) % owners) for d in range(owners)])

    block = jax.ShapeDtypeStruct((tokens + TAIL, part), bf16)
    cut = call(
        functools.partial(cut_kernel, n_dp),
        [block] * n_dp,
        cotangent,
        route_weight.reshape(1, tokens),
        expert_ids.reshape(1, tokens),
        slot_ids.reshape(1, tokens),
        name="cut",
    )
    blocks = [cut[0]] + [across(cut[mask], mask) for mask in range(1, n_dp)]

    def exchange(masks):
        size = len(masks) * capacity
        packed = call(
            functools.partial(pack_kernel, owners, capacity, len(masks)),
            [jax.ShapeDtypeStruct((size, part), bf16)] * owners,
            *[blocks[mask] for mask in masks],
            flops=2 * size * owners * tokens * part,
            name="pack",
        )
        return [packed[0]] + [along(packed[shift], shift) for shift in range(1, owners)]

    chunks = ((0, 1), (2, 3, 4, 5), (6, 7))
    arrived = [exchange(masks) for masks in chunks]

    half = ff // 2
    by_x, by_y = across(hidden, 2), across(hidden, 4)
    left, right = across(by_x[:, :half], 4), across(by_y[:, half:], 2)
    own = {0: [hidden], 2: [by_x], 4: [by_y], 6: [left, right]}
    rows = dict(own)
    for mask, parts in own.items():
        rows[mask ^ 1] = [across(p, 1) for p in parts]

    def operands(at):
        flat = list(arrived[at])
        for mask in chunks[at]:
            flat += rows[mask]
        return flat

    counts = [tuple(len(rows[mask]) for mask in masks) for masks in chunks]
    matrix = jax.ShapeDtypeStruct((part, ff), f32)
    early = call(
        functools.partial(early_kernel, owners, capacity, counts[:2]),
        matrix,
        *operands(0),
        *operands(1),
        flops=2 * 6 * owners * capacity * part * ff,
        name="early",
    )
    state = jax.ShapeDtypeStruct((1, part, ff), f32)
    new_first, new_second, update, sums = call(
        functools.partial(update_kernel, owners, capacity, counts[2:]),
        [state, state, matrix, jax.ShapeDtypeStruct((8, 128), f32)],
        *operands(2),
        early,
        down_weight,
        first_moment,
        second_moment,
        scratch=[pltpu.VMEM((part, ff), f32)],
        flops=2 * 2 * owners * capacity * part * ff,
        name="update",
    )
    sums = sums + across(sums, 1)
    parts = [sums] + [across(sums, mask) for mask in (2, 4, 6)]
    new_weight = call(
        functools.partial(weight_kernel, len(parts)),
        state,
        *parts,
        down_weight,
        update,
        name="weight",
    )
    return new_weight, new_first, new_second


def solution(mesh):
    placed = (
        P(("dp", "expert"), None),
        P(("dp", "expert")),
        P(("dp", "expert")),
        P(("dp", "expert")),
        P("dp", "expert", None, None, None),
        P("expert", "dp", None),
        P("expert", "dp", None),
        P("expert", "dp", None),
    )
    return jax.shard_map(
        by_permutes if mesh.shape["dp"] == 8 else on_device,
        mesh=mesh,
        in_specs=placed,
        out_specs=(P("expert", "dp", None), P("expert", "dp", None), P("expert", "dp", None)),
        check_vma=False,
    )
```

```python
import functools

import jax
import jax.numpy as jnp
from jax import lax
from jax.experimental import pallas as pl
from jax.experimental.pallas import tpu as pltpu
from jax.sharding import PartitionSpec as P

VMEM = pl.BlockSpec(memory_space=pltpu.VMEM)
TAIL = 16
ROWS_FIRST = (((0,), (0,)), ((), ()))


def on_device(
    cotangent,
    route_weight,
    expert_ids,
    slot_ids,
    hidden_saved,
    down_weight,
    first_moment,
    second_moment,
):
    tok_rows, width = cotangent.shape
    owners = lax.axis_size("expert")
    hidden_rows = hidden_saved.reshape(-1, hidden_saved.shape[-1])
    capacity = hidden_rows.shape[0] // owners
    weight = down_weight[0]
    routed = (route_weight[:, None] * cotangent.astype(jnp.float32)).astype(jnp.bfloat16)
    target = expert_ids * capacity + slot_ids
    outgoing = jnp.zeros((owners * capacity, width), jnp.bfloat16).at[target].set(routed)
    arrived = lax.all_to_all(
        outgoing.reshape(owners, capacity, width), "expert", split_axis=0, concat_axis=0, tiled=True
    )
    arrived = arrived.reshape(owners * capacity, width)
    whole_term = lax.dot_general(
        arrived, hidden_rows, (((0,), (0,)), ((), ())), preferred_element_type=jnp.float32
    )
    grad = lax.psum_scatter(whole_term, "dp", scatter_dimension=0, tiled=True)
    new_first = 0.9 * first_moment[0] + 0.1 * grad
    new_second = 0.999 * second_moment[0] + 0.001 * grad * grad
    update = (
        new_first / (1.0 - 0.9**10) / (jnp.sqrt(new_second / (1.0 - 0.999**10)) + 1e-06)
        + 0.01 * weight
    )
    weight_sq, update_sq = lax.psum((jnp.sum(weight * weight), jnp.sum(update * update)), "dp")
    ratio = jnp.sqrt(weight_sq) / (jnp.sqrt(update_sq) + 1e-06)
    new_weight = weight - 0.1 * ratio * update
    return (new_weight[None], new_first[None], new_second[None])


def cut_kernel(n_chips, cot_ref, scale_ref, expert_ref, slot_ref, *out_refs):
    tokens, width = cot_ref.shape
    part = width // n_chips
    half = part // 2
    me = lax.axis_index("dp")
    chip, core = me // 2, lax.rem(me, 2)
    scale = jnp.broadcast_to(scale_ref[...], (128, tokens)).T
    scale = jnp.concatenate([scale] * (half // 128), axis=1)
    row = lax.broadcasted_iota(jnp.int32, (TAIL, tokens), 0)
    ids = jnp.where(row == 0, expert_ref[...], jnp.where(row == 1, slot_ref[...], 0))
    ids = ids.astype(jnp.float32).astype(jnp.bfloat16)
    for mask, out_ref in enumerate(out_refs):
        for side in range(2):
            begin = (chip ^ mask) * part + (core ^ side) * half
            block = cot_ref[:, pl.ds(pl.multiple_of(begin, half), half)].astype(jnp.float32)
            out_ref[:tokens, side * half : (side + 1) * half] = (scale * block).astype(jnp.bfloat16)
        out_ref[tokens:, :] = jnp.concatenate([ids] * (part // tokens), axis=1)


def pack_kernel(owners, capacity, n_blocks, *refs):
    me = lax.axis_index("expert")
    blocks, outs = refs[:n_blocks], refs[n_blocks : n_blocks + owners]
    tokens = blocks[0].shape[0] - TAIL
    slot = lax.broadcasted_iota(jnp.int32, (capacity, tokens), 0).astype(jnp.float32)
    for at, block in enumerate(blocks):
        ids = block[tokens:, :tokens].astype(jnp.float32)
        place = ids[0:1, :] * capacity + ids[1:2, :]
        rows = block[:tokens, :]
        for shift, out in enumerate(outs):
            expert = lax.rem(me + shift, owners)
            first = (expert * capacity).astype(jnp.float32)
            hot = jnp.where(slot + first == place, 1.0, 0.0).astype(jnp.bfloat16)
            packed = jnp.dot(hot, rows, preferred_element_type=jnp.float32)
            out[at * capacity : (at + 1) * capacity, :] = packed.astype(jnp.bfloat16)


def product_kernel(owners, capacity, columns, cuts, *refs):
    me = lax.axis_index("expert")
    packed, refs = refs[:owners], refs[owners:]
    saved, early, out = refs[: sum(cuts)], refs[sum(cuts) : -1], refs[-1]
    begins = [
        pl.multiple_of(lax.rem(me + owners - shift, owners) * capacity, capacity) for shift in range(owners)
    ]
    rows = [
        jnp.concatenate([ref[at * capacity : (at + 1) * capacity, columns] for ref in packed])
        for at in range(len(cuts))
    ]
    groups = []
    for n in cuts:
        groups.append(saved[:n])
        saved = saved[n:]
    wide = min(part.shape[1] for parts in groups for part in parts)
    for column in range(0, out.shape[1], wide):
        total = None
        for group, parts in zip(rows, groups):
            part = parts[column // parts[0].shape[1]]
            inside = column % part.shape[1]
            right = jnp.concatenate([part[pl.ds(begin, capacity), inside : inside + wide] for begin in begins])
            term = lax.dot_general(group, right, ROWS_FIRST, preferred_element_type=jnp.float32)
            total = term if total is None else total + term
        for ref in early:
            total = total + ref[:, column : column + wide]
        out[:, column : column + wide] = total


def update_kernel(mine_ref, other_ref, weight_ref, first_ref, second_ref, new_first, new_second, update_ref, sums):
    grad = mine_ref[...] + other_ref[...]
    weight = weight_ref[0]
    first = 0.9 * first_ref[0] + 0.1 * grad
    second = 0.999 * second_ref[0] + 0.001 * grad * grad
    new_first[0] = first
    new_second[0] = second
    update = first / (1.0 - 0.9**10) / (jnp.sqrt(second / (1.0 - 0.999**10)) + 1e-06) + 0.01 * weight
    update_ref[...] = update
    row = lax.broadcasted_iota(jnp.int32, sums.shape, 0)
    sums[...] = jnp.where(row == 0, jnp.sum(weight * weight), jnp.sum(update * update))


def weight_kernel(n_sums, *refs):
    sums, (weight_ref, update_ref, new_weight) = refs[:n_sums], refs[n_sums:]
    total = sums[0][...]
    for other in sums[1:]:
        total = total + other[...]
    norm = jnp.sqrt(total)
    ratio = norm[0:1, 0:1] / (norm[1:2, 0:1] + 1e-06)
    new_weight[0] = weight_ref[0] - (0.1 * ratio) * update_ref[...]


def call(kernel, out_shape, *args, flops=0, name=None):
    nbytes = sum(a.size * a.dtype.itemsize for a in jax.tree.leaves((args, out_shape)))
    return pl.pallas_call(
        kernel,
        out_shape=out_shape,
        in_specs=[VMEM] * len(args),
        out_specs=jax.tree.map(lambda _: VMEM, out_shape),
        compiler_params=pltpu.CompilerParams(vmem_limit_bytes=40 * 2**20),
        cost_estimate=pl.CostEstimate(flops=flops, bytes_accessed=nbytes, transcendentals=0),
        name=name,
    )(*args)


def after(arrays, *earlier):
    return lax.optimization_barrier((arrays, earlier))[0]


def by_permutes(
    cotangent,
    route_weight,
    expert_ids,
    slot_ids,
    hidden_saved,
    down_weight,
    first_moment,
    second_moment,
):
    n_dp, owners = lax.axis_size("dp"), lax.axis_size("expert")
    n_chips = n_dp // 2
    tokens, width = cotangent.shape
    capacity, ff = hidden_saved.shape[3:]
    part = width // n_chips
    half = part // 2
    bf16, f32 = jnp.bfloat16, jnp.float32
    hidden = hidden_saved.reshape(owners * capacity, ff)

    def across(array, mask):
        return lax.ppermute(array, "dp", [(d, d ^ mask) for d in range(n_dp)])

    def along(array, shift):
        return lax.ppermute(array, "expert", [(d, (d + shift) % owners) for d in range(owners)])

    def pack(*blocks):
        size = len(blocks) * capacity
        return call(
            functools.partial(pack_kernel, owners, capacity, len(blocks)),
            [jax.ShapeDtypeStruct((size, part), bf16)] * owners,
            *blocks,
            flops=2 * size * owners * tokens * part,
            name="pack",
        )

    def multiply(columns, packed, groups, *early):
        n = columns.stop - columns.start
        return call(
            functools.partial(product_kernel, owners, capacity, columns, [len(parts) for parts in groups]),
            jax.ShapeDtypeStruct((n, ff), f32),
            *packed,
            *[part for parts in groups for part in parts],
            *early,
            flops=2 * len(groups) * owners * capacity * n * ff,
            name="product",
        )

    cut = call(
        functools.partial(cut_kernel, n_chips),
        [jax.ShapeDtypeStruct((tokens + TAIL, part), bf16)] * n_chips,
        cotangent,
        route_weight.reshape(1, tokens),
        expert_ids.reshape(1, tokens),
        slot_ids.reshape(1, tokens),
        name="cut",
    )
    near = pack(cut[0])
    cut = after((cut[1], cut[2], cut[3]), *near)
    from_x, from_y, from_xy = across(cut[0], 2), across(cut[1], 4), across(cut[2], 6)
    near = {0: near[0], 1: along(near[1], 1), 2: along(near[2], 2), 3: near[3]}
    near[3] = along(after(near[3], near[1]), 3)
    far = pack(from_x, from_y, from_xy)
    far, hidden_sent = after((far, hidden), *near.values())
    far = {0: far[0], 1: along(far[1], 1), 2: far[2], 3: along(far[3], 3)}
    by_x, by_y = across(hidden_sent, 2), across(hidden_sent, 4)
    far[2], left, right = after((far[2], by_x[:, : ff // 2], by_y[:, ff // 2 :]), far[1], far[3], by_x, by_y)
    far[2] = along(far[2], 2)
    by_xy = across(left, 4), across(right, 2)

    keep, give = slice(0, half), slice(half, part)
    totals = {}
    for side in (give, keep):
        early = multiply(side, near.values(), [(hidden,)])
        totals[side.start] = multiply(side, far.values(), [(by_x,), (by_y,), by_xy], early)
    other = across(totals[give.start], 1)

    state = jax.ShapeDtypeStruct((1, half, ff), f32)
    new_first, new_second, update, sums = call(
        update_kernel,
        [state, state, jax.ShapeDtypeStruct((half, ff), f32), jax.ShapeDtypeStruct((8, 128), f32)],
        totals[keep.start],
        other,
        down_weight,
        first_moment,
        second_moment,
        name="update",
    )
    sums = sums + across(sums, 1)
    parts = [sums] + [across(sums, mask) for mask in (2, 4, 6)]
    new_weight = call(
        functools.partial(weight_kernel, len(parts)),
        state,
        *parts,
        down_weight,
        update,
        name="weight",
    )
    return new_weight, new_first, new_second


def solution(mesh):
    placed = (
        P(("dp", "expert"), None),
        P(("dp", "expert")),
        P(("dp", "expert")),
        P(("dp", "expert")),
        P("dp", "expert", None, None, None),
        P("expert", "dp", None),
        P("expert", "dp", None),
        P("expert", "dp", None),
    )
    return jax.shard_map(
        by_permutes if mesh.shape["dp"] == 8 else on_device,
        mesh=mesh,
        in_specs=placed,
        out_specs=(P("expert", "dp", None), P("expert", "dp", None), P("expert", "dp", None)),
        check_vma=False,
    )
```

```python
import functools

import jax
import jax.numpy as jnp
from jax import lax
from jax.experimental import pallas as pl
from jax.experimental.pallas import tpu as pltpu
from jax.sharding import PartitionSpec as P

VMEM = pl.BlockSpec(memory_space=pltpu.VMEM)
HBM = pl.BlockSpec(memory_space=pltpu.HBM)
TAIL = 16
ROWS_FIRST = (((0,), (0,)), ((), ()))


def on_device(
    cotangent,
    route_weight,
    expert_ids,
    slot_ids,
    hidden_saved,
    down_weight,
    first_moment,
    second_moment,
):
    tok_rows, width = cotangent.shape
    owners = lax.axis_size("expert")
    hidden_rows = hidden_saved.reshape(-1, hidden_saved.shape[-1])
    capacity = hidden_rows.shape[0] // owners
    weight = down_weight[0]
    routed = (route_weight[:, None] * cotangent.astype(jnp.float32)).astype(jnp.bfloat16)
    target = expert_ids * capacity + slot_ids
    outgoing = jnp.zeros((owners * capacity, width), jnp.bfloat16).at[target].set(routed)
    arrived = lax.all_to_all(
        outgoing.reshape(owners, capacity, width), "expert", split_axis=0, concat_axis=0, tiled=True
    )
    arrived = arrived.reshape(owners * capacity, width)
    whole_term = lax.dot_general(
        arrived, hidden_rows, (((0,), (0,)), ((), ())), preferred_element_type=jnp.float32
    )
    grad = lax.psum_scatter(whole_term, "dp", scatter_dimension=0, tiled=True)
    new_first = 0.9 * first_moment[0] + 0.1 * grad
    new_second = 0.999 * second_moment[0] + 0.001 * grad * grad
    update = (
        new_first / (1.0 - 0.9**10) / (jnp.sqrt(new_second / (1.0 - 0.999**10)) + 1e-06)
        + 0.01 * weight
    )
    weight_sq, update_sq = lax.psum((jnp.sum(weight * weight), jnp.sum(update * update)), "dp")
    ratio = jnp.sqrt(weight_sq) / (jnp.sqrt(update_sq) + 1e-06)
    new_weight = weight - 0.1 * ratio * update
    return (new_weight[None], new_first[None], new_second[None])


def packed_rows(rows, expert_row, slot_row, expert, capacity):
    slot = lax.broadcasted_iota(jnp.int32, (capacity, rows.shape[0]), 0).astype(jnp.float32)
    place = (expert_row - expert.astype(jnp.float32)) * capacity + slot_row
    hot = jnp.where(slot == place, 1.0, 0.0).astype(jnp.bfloat16)
    return jnp.dot(hot, rows, preferred_element_type=jnp.float32).astype(jnp.bfloat16)


def cut_kernel(n_chips, owners, capacity, cot_ref, scale_ref, expert_ref, slot_ref, *refs):
    packed, blocks = refs[:owners], refs[owners : owners + n_chips - 1]
    cot, scales, experts, slots, sems = refs[owners + n_chips - 1 :]
    tokens, width = cot_ref.shape
    part = width // n_chips
    half = part // 2
    me = lax.axis_index("dp")
    chip, core = me // 2, lax.rem(me, 2)
    small = [
        pltpu.make_async_copy(src, dst, sems.at[at])
        for at, (src, dst) in enumerate([(scale_ref, scales), (expert_ref, experts), (slot_ref, slots)])
    ]
    large = []
    for mask in range(n_chips):
        columns = pl.ds(pl.multiple_of((chip ^ mask) * part, part), part)
        large.append(pltpu.make_async_copy(cot_ref.at[:, columns], cot.at[mask], sems.at[3 + mask]))
    for copy in small + large:
        copy.start()
    for copy in small:
        copy.wait()
    scale = jnp.broadcast_to(scales[...], (128, tokens)).T
    scale = jnp.concatenate([scale] * (half // 128), axis=1)
    expert_row, slot_row = experts[...].astype(jnp.float32), slots[...].astype(jnp.float32)
    row = lax.broadcasted_iota(jnp.int32, (TAIL, tokens), 0)
    ids = jnp.where(row == 0, expert_row, jnp.where(row == 1, slot_row, 0.0)).astype(jnp.bfloat16)
    for mask, copy in enumerate(large):
        copy.wait()
        halves = []
        for side in range(2):
            begin = pl.multiple_of((core ^ side) * half, half)
            block = cot[mask, :, pl.ds(begin, half)].astype(jnp.float32)
            halves.append((scale * block).astype(jnp.bfloat16))
        routed = jnp.concatenate(halves, axis=1)
        if mask == 0:
            z = lax.axis_index("expert")
            for shift, out in enumerate(packed):
                out[...] = packed_rows(routed, expert_row, slot_row, lax.rem(z + shift, owners), capacity)
        else:
            out = blocks[mask - 1]
            out[:tokens, :] = routed
            out[tokens:, :] = jnp.concatenate([ids] * (part // tokens), axis=1)


def pack_kernel(owners, capacity, n_blocks, *refs):
    z = lax.axis_index("expert")
    blocks, outs = refs[:n_blocks], refs[n_blocks:]
    tokens = blocks[0].shape[0] - TAIL
    for at, block in enumerate(blocks):
        ids = block[tokens:, :tokens].astype(jnp.float32)
        rows = block[:tokens, :]
        for shift, out in enumerate(outs):
            expert = lax.rem(z + shift, owners)
            out[at * capacity : (at + 1) * capacity, :] = packed_rows(rows, ids[0:1], ids[1:2], expert, capacity)


def product_kernel(owners, capacity, columns, plan, *refs):
    me = lax.axis_index("expert")
    used = 1 + max(max(max(parts), max(place for place, _, _ in packed)) for parts, packed in plan)
    early, out = refs[used:-1], refs[-1]
    rows = [
        jnp.concatenate([refs[place][at * capacity : (at + 1) * capacity, columns] for place, at, _ in packed])
        for _, packed in plan
    ]
    wide = min(refs[place].shape[1] for parts, _ in plan for place in parts)
    for column in range(0, out.shape[1], wide):
        total = None
        for left, (parts, packed) in zip(rows, plan):
            part = refs[parts[column // refs[parts[0]].shape[1]]]
            inside = slice(column % part.shape[1], column % part.shape[1] + wide)
            begins = [lax.rem(me + owners - shift, owners) * capacity for _, _, shift in packed]
            right = [part[pl.ds(pl.multiple_of(begin, capacity), capacity), inside] for begin in begins]
            term = lax.dot_general(left, jnp.concatenate(right), ROWS_FIRST, preferred_element_type=jnp.float32)
            total = term if total is None else total + term
        for ref in early:
            total = total + ref[:, column : column + wide]
        out[:, column : column + wide] = total


def new_moments(grad, first_ref, second_ref):
    return 0.9 * first_ref[0] + 0.1 * grad, 0.999 * second_ref[0] + 0.001 * grad * grad


def update_kernel(mine_ref, other_ref, weight_ref, first_ref, second_ref, grad_ref, update_ref, sums):
    grad = mine_ref[...] + other_ref[...]
    grad_ref[...] = grad
    weight = weight_ref[0]
    first, second = new_moments(grad, first_ref, second_ref)
    update = first / (1.0 - 0.9**10) / (jnp.sqrt(second / (1.0 - 0.999**10)) + 1e-06) + 0.01 * weight
    update_ref[...] = update
    row = lax.broadcasted_iota(jnp.int32, sums.shape, 0)
    sums[...] = jnp.where(row == 0, jnp.sum(weight * weight), jnp.sum(update * update))


def moment_kernel(grad_ref, first_ref, second_ref, new_first, new_second):
    new_first[0], new_second[0] = new_moments(grad_ref[...], first_ref, second_ref)


def weight_kernel(n_sums, *refs):
    sums, (weight_ref, update_ref, out_ref, new_weight, sems) = refs[:n_sums], refs[n_sums:]
    total = sums[0][...]
    for other in sums[1:]:
        total = total + other[...]
    norm = jnp.sqrt(total)
    scale = 0.1 * (norm[0:1, 0:1] / (norm[1:2, 0:1] + 1e-06))
    n = sems.shape[0]
    rows = update_ref.shape[0] // n
    copies = []
    for at in range(n):
        span = pl.ds(at * rows, rows)
        new_weight[0, span, :] = weight_ref[0, span, :] - scale * update_ref[span, :]
        copies.append(pltpu.make_async_copy(new_weight.at[:, span], out_ref.at[:, span], sems.at[at]))
        copies[-1].start()
    for copy in copies:
        copy.wait()


def call(kernel, out_shape, *args, spaces=VMEM, out_spaces=VMEM, scratch=(), grant=40, flops=0, name=None):
    nbytes = sum(a.size * a.dtype.itemsize for a in jax.tree.leaves((args, out_shape)))
    return pl.pallas_call(
        kernel,
        out_shape=out_shape,
        in_specs=[spaces] * len(args),
        out_specs=jax.tree.map(lambda _: out_spaces, out_shape),
        scratch_shapes=scratch,
        compiler_params=pltpu.CompilerParams(vmem_limit_bytes=grant * 2**20),
        cost_estimate=pl.CostEstimate(flops=flops, bytes_accessed=nbytes, transcendentals=0),
        name=name,
    )(*args)


def after(arrays, *earlier):
    return lax.optimization_barrier((arrays, earlier))[0]


def by_permutes(
    cotangent,
    route_weight,
    expert_ids,
    slot_ids,
    hidden_saved,
    down_weight,
    first_moment,
    second_moment,
):
    n_dp, owners = lax.axis_size("dp"), lax.axis_size("expert")
    n_chips = n_dp // 2
    tokens, width = cotangent.shape
    capacity, ff = hidden_saved.shape[3:]
    part = width // n_chips
    half = part // 2
    bf16, f32 = jnp.bfloat16, jnp.float32
    hidden = hidden_saved.reshape(owners * capacity, ff)

    def across(array, mask):
        return lax.ppermute(array, "dp", [(d, d ^ mask) for d in range(n_dp)])

    def along(array, shift):
        return lax.ppermute(array, "expert", [(d, (d + shift) % owners) for d in range(owners)])

    def pack(*blocks):
        size = len(blocks) * capacity
        return call(
            functools.partial(pack_kernel, owners, capacity, len(blocks)),
            [jax.ShapeDtypeStruct((size, part), bf16)] * owners,
            *blocks,
            flops=2 * size * owners * tokens * part,
            name="pack",
        )

    def multiply(columns, groups, *early):
        arrays, plan = [], []

        def place(array):
            if not any(array is other for other in arrays):
                arrays.append(array)
            return [array is other for other in arrays].index(True)

        for parts, packed in groups:
            plan.append(([place(p) for p in parts], [(place(p), at, shift) for p, at, shift in packed]))
        n = columns.stop - columns.start
        return call(
            functools.partial(product_kernel, owners, capacity, columns, plan),
            jax.ShapeDtypeStruct((n, ff), f32),
            *arrays,
            *early,
            flops=2 * sum(len(packed) for _, packed in plan) * capacity * n * ff,
            name="product",
        )

    packed, block = jax.ShapeDtypeStruct((capacity, part), bf16), jax.ShapeDtypeStruct((tokens + TAIL, part), bf16)
    cut = call(
        functools.partial(cut_kernel, n_chips, owners, capacity),
        [packed] * owners + [block] * (n_chips - 1),
        cotangent,
        *[ids.reshape(1, tokens) for ids in (route_weight, expert_ids, slot_ids)],
        spaces=HBM,
        scratch=[
            pltpu.VMEM((n_chips, tokens, part), bf16),
            pltpu.VMEM((1, tokens), f32),
            pltpu.VMEM((1, tokens), jnp.int32),
            pltpu.VMEM((1, tokens), jnp.int32),
            pltpu.SemaphoreType.DMA((3 + n_chips,)),
        ],
        grant=60,
        name="cut",
    )
    near, (to_x, to_y, to_xy) = cut[:owners], cut[owners:]
    from_x, from_y, from_xy = across(to_x, 2), across(to_y, 4), across(to_xy, 6)
    near = [near[0], along(near[1], 1), along(near[2], 2), near[3]]
    near[3] = along(after(near[3], near[1]), 3)
    far = pack(from_x, from_y, from_xy)
    far, left, right = after((far, hidden[:, : ff // 2], hidden[:, ff // 2 :]), *near)
    far = list(far)
    x_left, x_right, y_left, y_right = across(left, 2), across(right, 2), across(left, 4), across(right, 4)
    far[2] = along(far[2], 2)
    far[1], far[3], xy_left, xy_right = after(
        (far[1], far[3], x_left, y_right), far[2], x_left, x_right, y_left, y_right
    )
    far[1], far[3] = along(far[1], 1), along(far[3], 3)
    xy_left, xy_right = across(xy_left, 4), across(xy_right, 2)

    keep, give = slice(0, half), slice(half, part)
    def terms(packed, at, *shifts):
        return [(packed[shift], at, shift) for shift in shifts]

    by_x, by_y, by_xy = (x_left, x_right), (y_left, y_right), (xy_left, xy_right)
    totals = {}
    for side in (give, keep):
        groups = [((hidden,), terms(near, 0, 0, 1, 2, 3)), (by_x, terms(far, 0, 0, 2)), (by_y, terms(far, 1, 0, 2))]
        totals[side.start] = multiply(side, groups)
    totals = after(totals, *totals.values())
    for side in (give, keep):
        groups = [(by_x, terms(far, 0, 1, 3)), (by_y, terms(far, 1, 1, 3)), (by_xy, terms(far, 2, 0, 1, 2, 3))]
        totals[side.start] = multiply(side, groups, totals[side.start])
    other = across(totals[give.start], 1)

    state, matrix = jax.ShapeDtypeStruct((1, half, ff), f32), jax.ShapeDtypeStruct((half, ff), f32)
    grad, update, sums = call(
        update_kernel,
        [matrix, matrix, jax.ShapeDtypeStruct((8, 128), f32)],
        totals[keep.start],
        other,
        down_weight,
        first_moment,
        second_moment,
        name="update",
    )
    sums = sums + across(sums, 1)
    parts = [sums] + [across(sums, mask) for mask in (2, 4, 6)]
    new_first, new_second = call(
        moment_kernel, [state, state], after(grad, sums), first_moment, second_moment, name="moment"
    )
    new_weight = call(
        functools.partial(weight_kernel, len(parts)),
        state,
        *parts,
        down_weight,
        update,
        out_spaces=HBM,
        scratch=[pltpu.VMEM((1, half, ff), f32), pltpu.SemaphoreType.DMA((4,))],
        name="weight",
    )
    return new_weight, new_first, new_second


def solution(mesh):
    placed = (
        P(("dp", "expert"), None),
        P(("dp", "expert")),
        P(("dp", "expert")),
        P(("dp", "expert")),
        P("dp", "expert", None, None, None),
        P("expert", "dp", None),
        P("expert", "dp", None),
        P("expert", "dp", None),
    )
    return jax.shard_map(
        by_permutes if mesh.shape["dp"] == 8 else on_device,
        mesh=mesh,
        in_specs=placed,
        out_specs=(P("expert", "dp", None), P("expert", "dp", None), P("expert", "dp", None)),
        check_vma=False,
    )
```

```python
import functools

import jax
import jax.numpy as jnp
from jax import lax
from jax.experimental import pallas as pl
from jax.experimental.pallas import tpu as pltpu
from jax.sharding import PartitionSpec as P

VMEM = pl.BlockSpec(memory_space=pltpu.VMEM)
HBM = pl.BlockSpec(memory_space=pltpu.HBM)
TAIL = 16
ROWS_FIRST = (((0,), (0,)), ((), ()))


def on_device(
    cotangent,
    route_weight,
    expert_ids,
    slot_ids,
    hidden_saved,
    down_weight,
    first_moment,
    second_moment,
):
    tok_rows, width = cotangent.shape
    owners = lax.axis_size("expert")
    hidden_rows = hidden_saved.reshape(-1, hidden_saved.shape[-1])
    capacity = hidden_rows.shape[0] // owners
    weight = down_weight[0]
    routed = (route_weight[:, None] * cotangent.astype(jnp.float32)).astype(jnp.bfloat16)
    target = expert_ids * capacity + slot_ids
    outgoing = jnp.zeros((owners * capacity, width), jnp.bfloat16).at[target].set(routed)
    arrived = lax.all_to_all(
        outgoing.reshape(owners, capacity, width), "expert", split_axis=0, concat_axis=0, tiled=True
    )
    arrived = arrived.reshape(owners * capacity, width)
    whole_term = lax.dot_general(
        arrived, hidden_rows, (((0,), (0,)), ((), ())), preferred_element_type=jnp.float32
    )
    grad = lax.psum_scatter(whole_term, "dp", scatter_dimension=0, tiled=True)
    new_first = 0.9 * first_moment[0] + 0.1 * grad
    new_second = 0.999 * second_moment[0] + 0.001 * grad * grad
    update = (
        new_first / (1.0 - 0.9**10) / (jnp.sqrt(new_second / (1.0 - 0.999**10)) + 1e-06)
        + 0.01 * weight
    )
    weight_sq, update_sq = lax.psum((jnp.sum(weight * weight), jnp.sum(update * update)), "dp")
    ratio = jnp.sqrt(weight_sq) / (jnp.sqrt(update_sq) + 1e-06)
    new_weight = weight - 0.1 * ratio * update
    return (new_weight[None], new_first[None], new_second[None])


def packed_rows(rows, expert_row, slot_row, expert, capacity):
    slot = lax.broadcasted_iota(jnp.int32, (capacity, rows.shape[0]), 0).astype(jnp.float32)
    place = (expert_row - expert.astype(jnp.float32)) * capacity + slot_row
    hot = jnp.where(slot == place, 1.0, 0.0).astype(jnp.bfloat16)
    return jnp.dot(hot, rows, preferred_element_type=jnp.float32).astype(jnp.bfloat16)


def cut_kernel(n_chips, owners, capacity, cot_ref, scale_ref, expert_ref, slot_ref, *refs):
    packed, blocks = refs[:owners], refs[owners : owners + n_chips - 1]
    cot, scales, experts, slots, out_packed, out_blocks, sems, out_sems = refs[owners + n_chips - 1 :]
    tokens, width = cot_ref.shape
    part = width // n_chips
    half = part // 2
    me = lax.axis_index("dp")
    chip, core = me // 2, lax.rem(me, 2)
    small = [
        pltpu.make_async_copy(src, dst, sems.at[at])
        for at, (src, dst) in enumerate([(scale_ref, scales), (expert_ref, experts), (slot_ref, slots)])
    ]
    large = []
    for mask in range(n_chips):
        columns = pl.ds(pl.multiple_of((chip ^ mask) * part, part), part)
        large.append(pltpu.make_async_copy(cot_ref.at[:, columns], cot.at[mask], sems.at[3 + mask]))
    order = (*range(1, n_chips), 0)
    for copy in small + [large[mask] for mask in order]:
        copy.start()
    for copy in small:
        copy.wait()
    scale = jnp.broadcast_to(scales[...], (128, tokens)).T
    scale = jnp.concatenate([scale] * (half // 128), axis=1)
    expert_row, slot_row = experts[...].astype(jnp.float32), slots[...].astype(jnp.float32)
    row = lax.broadcasted_iota(jnp.int32, (TAIL, tokens), 0)
    ids = jnp.where(row == 0, expert_row, jnp.where(row == 1, slot_row, 0.0)).astype(jnp.bfloat16)
    out_copies = []

    def send(src, dst):
        copy = pltpu.make_async_copy(src, dst, out_sems.at[len(out_copies)])
        copy.start()
        out_copies.append(copy)

    for mask in order:
        large[mask].wait()
        halves = []
        for side in range(2):
            begin = pl.multiple_of((core ^ side) * half, half)
            block = cot[mask, :, pl.ds(begin, half)].astype(jnp.float32)
            halves.append((scale * block).astype(jnp.bfloat16))
        routed = jnp.concatenate(halves, axis=1)
        if mask:
            out_blocks[mask - 1, :tokens, :] = routed
            out_blocks[mask - 1, tokens:, :] = jnp.concatenate([ids] * (part // tokens), axis=1)
            send(out_blocks.at[mask - 1], blocks[mask - 1])
        else:
            z = lax.axis_index("expert")
            for shift, out in enumerate(packed):
                expert = lax.rem(z + shift, owners)
                out_packed[shift] = packed_rows(routed, expert_row, slot_row, expert, capacity)
                send(out_packed.at[shift], out)
    for copy in out_copies:
        copy.wait()


def pack_kernel(owners, capacity, n_blocks, *refs):
    z = lax.axis_index("expert")
    blocks, outs = refs[:n_blocks], refs[n_blocks:]
    tokens = blocks[0].shape[0] - TAIL
    for at, block in enumerate(blocks):
        ids = block[tokens:, :tokens].astype(jnp.float32)
        rows = block[:tokens, :]
        for shift, out in enumerate(outs):
            expert = lax.rem(z + shift, owners)
            out[at * capacity : (at + 1) * capacity, :] = packed_rows(rows, ids[0:1], ids[1:2], expert, capacity)


def product_kernel(owners, capacity, columns, first, plan, *refs):
    me = lax.axis_index("expert")
    used = 1 + max(max(max(parts), max(place for place, _, _ in packed)) for parts, packed in plan)
    early, out = refs[used:-1], refs[-1]
    rows = [
        jnp.concatenate([refs[place][at * capacity : (at + 1) * capacity, columns] for place, at, _ in packed])
        for _, packed in plan
    ]
    wide = min(refs[place].shape[1] for parts, _ in plan for place in parts)
    for column in range(first, first + out.shape[1], wide):
        total = None
        for left, (parts, packed) in zip(rows, plan):
            part = refs[parts[column // refs[parts[0]].shape[1]]]
            inside = slice(column % part.shape[1], column % part.shape[1] + wide)
            begins = [lax.rem(me + owners - shift, owners) * capacity for _, _, shift in packed]
            right = [part[pl.ds(pl.multiple_of(begin, capacity), capacity), inside] for begin in begins]
            term = lax.dot_general(left, jnp.concatenate(right), ROWS_FIRST, preferred_element_type=jnp.float32)
            total = term if total is None else total + term
        for ref in early:
            total = total + ref[:, column : column + wide]
        out[:, column - first : column - first + wide] = total


def new_moments(grad, first_ref, second_ref):
    return 0.9 * first_ref[0] + 0.1 * grad, 0.999 * second_ref[0] + 0.001 * grad * grad


def update_kernel(mine_ref, left_ref, right_ref, weight_ref, first_ref, second_ref, grad_ref, update_ref, sums):
    grad = mine_ref[...] + jnp.concatenate([left_ref[...], right_ref[...]], axis=1)
    grad_ref[...] = grad
    weight = weight_ref[0]
    first, second = new_moments(grad, first_ref, second_ref)
    first, second = first * (1.0 / (1.0 - 0.9**10)), second * (1.0 / (1.0 - 0.999**10))
    root = second * lax.rsqrt(second)
    update = first * pl.reciprocal(root + 1e-06) + 0.01 * weight
    update_ref[...] = update
    row = lax.broadcasted_iota(jnp.int32, sums.shape, 0)
    sums[...] = jnp.where(row == 0, jnp.sum(weight * weight), jnp.sum(update * update))


def moment_kernel(grad_ref, first_ref, second_ref, new_first, new_second):
    new_first[0], new_second[0] = new_moments(grad_ref[...], first_ref, second_ref)


def weight_kernel(n_sums, *refs):
    sums, (weight_ref, update_ref, out_ref, new_weight, sems) = refs[:n_sums], refs[n_sums:]
    total = sums[0][...]
    for other in sums[1:]:
        total = total + other[...]
    norm = jnp.sqrt(total)
    scale = 0.1 * (norm[0:1, 0:1] / (norm[1:2, 0:1] + 1e-06))
    n = sems.shape[0]
    rows = update_ref.shape[0] // n
    copies = []
    for at in range(n):
        span = pl.ds(at * rows, rows)
        new_weight[0, span, :] = weight_ref[0, span, :] - scale * update_ref[span, :]
        copies.append(pltpu.make_async_copy(new_weight.at[:, span], out_ref.at[:, span], sems.at[at]))
        copies[-1].start()
    for copy in copies:
        copy.wait()


def call(kernel, out_shape, *args, spaces=VMEM, out_spaces=VMEM, scratch=(), grant=40, flops=0, name=None):
    nbytes = sum(a.size * a.dtype.itemsize for a in jax.tree.leaves((args, out_shape)))
    return pl.pallas_call(
        kernel,
        out_shape=out_shape,
        in_specs=[spaces] * len(args),
        out_specs=jax.tree.map(lambda _: out_spaces, out_shape),
        scratch_shapes=scratch,
        compiler_params=pltpu.CompilerParams(vmem_limit_bytes=grant * 2**20),
        cost_estimate=pl.CostEstimate(flops=flops, bytes_accessed=nbytes, transcendentals=0),
        name=name,
    )(*args)


def after(arrays, *earlier):
    return lax.optimization_barrier((arrays, earlier))[0]


def by_permutes(
    cotangent,
    route_weight,
    expert_ids,
    slot_ids,
    hidden_saved,
    down_weight,
    first_moment,
    second_moment,
):
    n_dp, owners = lax.axis_size("dp"), lax.axis_size("expert")
    n_chips = n_dp // 2
    tokens, width = cotangent.shape
    capacity, ff = hidden_saved.shape[3:]
    part = width // n_chips
    half = part // 2
    bf16, f32 = jnp.bfloat16, jnp.float32
    hidden = hidden_saved.reshape(owners * capacity, ff)

    def across(array, mask):
        return lax.ppermute(array, "dp", [(d, d ^ mask) for d in range(n_dp)])

    def along(array, shift):
        return lax.ppermute(array, "expert", [(d, (d + shift) % owners) for d in range(owners)])

    def pack(*blocks):
        size = len(blocks) * capacity
        return call(
            functools.partial(pack_kernel, owners, capacity, len(blocks)),
            [jax.ShapeDtypeStruct((size, part), bf16)] * owners,
            *blocks,
            flops=4 * 2 * size * owners * tokens * part,
            name="pack",
        )

    def multiply(columns, groups, *early, span=slice(0, ff)):
        arrays, plan = [], []

        def place(array):
            if not any(array is other for other in arrays):
                arrays.append(array)
            return [array is other for other in arrays].index(True)

        for parts, packed in groups:
            plan.append(([place(p) for p in parts], [(place(p), at, shift) for p, at, shift in packed]))
        n = columns.stop - columns.start
        return call(
            functools.partial(product_kernel, owners, capacity, columns, span.start, plan),
            jax.ShapeDtypeStruct((n, span.stop - span.start), f32),
            *arrays,
            *early,
            flops=2 * sum(len(packed) for _, packed in plan) * capacity * n * (span.stop - span.start),
            name="product",
        )

    packed, block = jax.ShapeDtypeStruct((capacity, part), bf16), jax.ShapeDtypeStruct((tokens + TAIL, part), bf16)
    cut = call(
        functools.partial(cut_kernel, n_chips, owners, capacity),
        [packed] * owners + [block] * (n_chips - 1),
        cotangent,
        *[ids.reshape(1, tokens) for ids in (route_weight, expert_ids, slot_ids)],
        spaces=HBM,
        scratch=[
            pltpu.VMEM((n_chips, tokens, part), bf16),
            pltpu.VMEM((1, tokens), f32),
            pltpu.VMEM((1, tokens), jnp.int32),
            pltpu.VMEM((1, tokens), jnp.int32),
            pltpu.VMEM((owners, capacity, part), bf16),
            pltpu.VMEM((n_chips - 1, tokens + TAIL, part), bf16),
            pltpu.SemaphoreType.DMA((3 + n_chips,)),
            pltpu.SemaphoreType.DMA((owners + n_chips - 1,)),
        ],
        out_spaces=HBM,
        grant=60,
        name="cut",
    )
    near, (to_x, to_y, to_xy) = cut[:owners], cut[owners:]
    from_x, from_y, from_xy = across(to_x, 2), across(to_y, 4), across(to_xy, 6)
    near = [near[0], along(near[1], 1), along(near[2], 2), near[3]]
    near[3] = along(after(near[3], near[1]), 3)
    far = pack(from_x, from_y, from_xy)
    far, left, right = after((far, hidden[:, : ff // 2], hidden[:, ff // 2 :]), *near)
    far = list(far)
    x_left, x_right, y_left, y_right = across(left, 2), across(right, 2), across(left, 4), across(right, 4)
    far[2] = along(far[2], 2)
    far[1], far[3], xy_left, xy_right = after(
        (far[1], far[3], x_left, y_right), far[2], x_left, x_right, y_left, y_right
    )
    far[1], far[3] = along(far[1], 1), along(far[3], 3)
    xy_left, xy_right = across(xy_left, 4), across(xy_right, 2)

    keep, give = slice(0, half), slice(half, part)
    def terms(packed, at, *shifts):
        return [(packed[shift], at, shift) for shift in shifts]

    by_x, by_y, by_xy = (x_left, x_right), (y_left, y_right), (xy_left, xy_right)
    totals = {}
    for side in (give, keep):
        groups = [((hidden,), terms(near, 0, 0, 1, 2, 3)), (by_x, terms(far, 0, 0, 2)), (by_y, terms(far, 1, 0, 2))]
        totals[side.start] = multiply(side, groups)
    totals = after(totals, *totals.values())
    for side in (give, keep):
        groups = [(by_x, terms(far, 0, 1)), (by_y, terms(far, 1, 1))]
        totals[side.start] = multiply(side, groups, totals[side.start])
    totals = after(totals, *totals.values())
    groups = [(by_x, terms(far, 0, 3)), (by_y, terms(far, 1, 3)), (by_xy, terms(far, 2, 0, 1, 2, 3))]
    spans = slice(0, ff // 2), slice(ff // 2, ff)
    given = [multiply(give, groups, totals[give.start], span=span) for span in spans]
    other = [across(part, 1) for part in given]
    kept = multiply(keep, groups, after(totals[keep.start], *given))

    state, matrix = jax.ShapeDtypeStruct((1, half, ff), f32), jax.ShapeDtypeStruct((half, ff), f32)
    grad, update, sums = call(
        update_kernel,
        [matrix, matrix, jax.ShapeDtypeStruct((8, 128), f32)],
        kept,
        *other,
        down_weight,
        first_moment,
        second_moment,
        name="update",
    )
    sums = sums + across(sums, 1)
    parts = [sums] + [across(sums, mask) for mask in (2, 4, 6)]
    new_first, new_second = call(
        moment_kernel, [state, state], after(grad, sums), first_moment, second_moment, name="moment"
    )
    new_weight = call(
        functools.partial(weight_kernel, len(parts)),
        state,
        *parts,
        down_weight,
        update,
        out_spaces=HBM,
        scratch=[pltpu.VMEM((1, half, ff), f32), pltpu.SemaphoreType.DMA((4,))],
        name="weight",
    )
    return new_weight, new_first, new_second


def solution(mesh):
    placed = (
        P(("dp", "expert"), None),
        P(("dp", "expert")),
        P(("dp", "expert")),
        P(("dp", "expert")),
        P("dp", "expert", None, None, None),
        P("expert", "dp", None),
        P("expert", "dp", None),
        P("expert", "dp", None),
    )
    return jax.shard_map(
        by_permutes if mesh.shape["dp"] == 8 else on_device,
        mesh=mesh,
        in_specs=placed,
        out_specs=(P("expert", "dp", None), P("expert", "dp", None), P("expert", "dp", None)),
        check_vma=False,
    )
```

```python
import functools

import jax
import jax.numpy as jnp
from jax import lax
from jax.experimental import pallas as pl
from jax.experimental.pallas import tpu as pltpu
from jax.sharding import PartitionSpec as P

VMEM = pl.BlockSpec(memory_space=pltpu.VMEM)
HBM = pl.BlockSpec(memory_space=pltpu.HBM)
ANY = pl.BlockSpec(memory_space=pl.ANY)
TAIL = 16
ROWS_FIRST = (((0,), (0,)), ((), ()))


def on_device(
    cotangent,
    route_weight,
    expert_ids,
    slot_ids,
    hidden_saved,
    down_weight,
    first_moment,
    second_moment,
):
    tok_rows, width = cotangent.shape
    owners = lax.axis_size("expert")
    hidden_rows = hidden_saved.reshape(-1, hidden_saved.shape[-1])
    capacity = hidden_rows.shape[0] // owners
    weight = down_weight[0]
    routed = (route_weight[:, None] * cotangent.astype(jnp.float32)).astype(jnp.bfloat16)
    target = expert_ids * capacity + slot_ids
    outgoing = jnp.zeros((owners * capacity, width), jnp.bfloat16).at[target].set(routed)
    arrived = lax.all_to_all(
        outgoing.reshape(owners, capacity, width), "expert", split_axis=0, concat_axis=0, tiled=True
    )
    arrived = arrived.reshape(owners * capacity, width)
    whole_term = lax.dot_general(
        arrived, hidden_rows, (((0,), (0,)), ((), ())), preferred_element_type=jnp.float32
    )
    grad = lax.psum_scatter(whole_term, "dp", scatter_dimension=0, tiled=True)
    new_first = 0.9 * first_moment[0] + 0.1 * grad
    new_second = 0.999 * second_moment[0] + 0.001 * grad * grad
    update = (
        new_first / (1.0 - 0.9**10) / (jnp.sqrt(new_second / (1.0 - 0.999**10)) + 1e-06)
        + 0.01 * weight
    )
    weight_sq, update_sq = lax.psum((jnp.sum(weight * weight), jnp.sum(update * update)), "dp")
    ratio = jnp.sqrt(weight_sq) / (jnp.sqrt(update_sq) + 1e-06)
    new_weight = weight - 0.1 * ratio * update
    return (new_weight[None], new_first[None], new_second[None])


def packed_rows(rows, expert_row, slot_row, expert, capacity):
    slot = lax.broadcasted_iota(jnp.int32, (capacity, rows.shape[0]), 0).astype(jnp.float32)
    place = (expert_row - expert.astype(jnp.float32)) * capacity + slot_row
    hot = jnp.where(slot == place, 1.0, 0.0).astype(jnp.bfloat16)
    return jnp.dot(hot, rows, preferred_element_type=jnp.float32).astype(jnp.bfloat16)


def cut_kernel(n_chips, owners, capacity, cot_ref, scale_ref, expert_ref, slot_ref, *refs):
    packed, blocks = refs[:owners], refs[owners : owners + n_chips - 1]
    cot, scales, experts, slots, sems = refs[owners + n_chips - 1 :]
    tokens, width = cot_ref.shape
    part = width // n_chips
    half = part // 2
    me = lax.axis_index("dp")
    chip, core = me // 2, lax.rem(me, 2)
    small = [
        pltpu.make_async_copy(src, dst, sems.at[at])
        for at, (src, dst) in enumerate([(scale_ref, scales), (expert_ref, experts), (slot_ref, slots)])
    ]
    large = []
    for mask in range(n_chips):
        columns = pl.ds(pl.multiple_of((chip ^ mask) * part, part), part)
        large.append(pltpu.make_async_copy(cot_ref.at[:, columns], cot.at[mask], sems.at[3 + mask]))
    order = (*range(1, n_chips), 0)
    for copy in small + [large[mask] for mask in order]:
        copy.start()
    for copy in small:
        copy.wait()
    scale = jnp.broadcast_to(scales[...], (128, tokens)).T
    scale = jnp.concatenate([scale] * (half // 128), axis=1)
    expert_row, slot_row = experts[...].astype(jnp.float32), slots[...].astype(jnp.float32)
    row = lax.broadcasted_iota(jnp.int32, (TAIL, tokens), 0)
    ids = jnp.where(row == 0, expert_row, jnp.where(row == 1, slot_row, 0.0)).astype(jnp.bfloat16)
    for mask in order:
        large[mask].wait()
        halves = []
        for side in range(2):
            begin = pl.multiple_of((core ^ side) * half, half)
            block = cot[mask, :, pl.ds(begin, half)].astype(jnp.float32)
            halves.append((scale * block).astype(jnp.bfloat16))
        routed = jnp.concatenate(halves, axis=1)
        if mask:
            out = blocks[mask - 1]
            out[:tokens, :] = routed
            out[tokens:, :] = jnp.concatenate([ids] * (part // tokens), axis=1)
        else:
            z = lax.axis_index("expert")
            for shift, out in enumerate(packed):
                expert = lax.rem(z + shift, owners)
                out[...] = packed_rows(routed, expert_row, slot_row, expert, capacity)


def pack_kernel(owners, capacity, n_blocks, *refs):
    z = lax.axis_index("expert")
    blocks, outs = refs[:n_blocks], refs[n_blocks:]
    tokens = blocks[0].shape[0] - TAIL
    for at, block in enumerate(blocks):
        ids = block[tokens:, :tokens].astype(jnp.float32)
        rows = block[:tokens, :]
        for shift, out in enumerate(outs):
            expert = lax.rem(z + shift, owners)
            out[at * capacity : (at + 1) * capacity, :] = packed_rows(rows, ids[0:1], ids[1:2], expert, capacity)


def product_kernel(owners, capacity, columns, first, plan, n_early, *refs):
    me = lax.axis_index("expert")
    used = 1 + max(max(max(parts), max(place for place, _, _ in packed)) for parts, packed in plan)
    early, out = refs[used : used + n_early], refs[-1]
    rows = [
        jnp.concatenate([refs[place][at * capacity : (at + 1) * capacity, columns] for place, at, _ in packed])
        for _, packed in plan
    ]
    wide = min(out.shape[1], *(refs[place].shape[1] for parts, _ in plan for place in parts))
    for column in range(first, first + out.shape[1], wide):
        total = None
        for left, (parts, packed) in zip(rows, plan):
            size = refs[parts[0]].shape[1]
            part = refs[parts[column // size]]
            inside = slice(column % size, column % size + wide)
            begins = [lax.rem(me + owners - shift, owners) * capacity for _, _, shift in packed]
            right = [part[pl.ds(pl.multiple_of(begin, capacity), capacity), inside] for begin in begins]
            term = lax.dot_general(left, jnp.concatenate(right), ROWS_FIRST, preferred_element_type=jnp.float32)
            total = term if total is None else total + term
        for ref in early:
            total = total + ref[:, column : column + wide]
        out[:, column - first : column - first + wide] = total


def new_moments(grad, first_ref, second_ref):
    return 0.9 * first_ref[0] + 0.1 * grad, 0.999 * second_ref[0] + 0.001 * grad * grad


def update_kernel(mine_ref, left_ref, right_ref, weight_ref, first_ref, second_ref, grad_ref, update_ref, sums):
    grad = mine_ref[...] + jnp.concatenate([left_ref[...], right_ref[...]], axis=1)
    grad_ref[...] = grad
    weight = weight_ref[0]
    first, second = new_moments(grad, first_ref, second_ref)
    first, second = first * (1.0 / (1.0 - 0.9**10)), second * (1.0 / (1.0 - 0.999**10))
    root = second * lax.rsqrt(second)
    update = first * pl.reciprocal(root + 1e-06) + 0.01 * weight
    update_ref[...] = update
    row = lax.broadcasted_iota(jnp.int32, sums.shape, 0)
    sums[...] = jnp.where(row == 0, jnp.sum(weight * weight), jnp.sum(update * update))


def moment_kernel(grad_ref, first_ref, second_ref, new_first, new_second):
    new_first[0], new_second[0] = new_moments(grad_ref[...], first_ref, second_ref)


def weight_kernel(n_sums, *refs):
    sums, (weight_ref, update_ref, out_ref, new_weight, sems) = refs[:n_sums], refs[n_sums:]
    total = sums[0][...]
    for other in sums[1:]:
        total = total + other[...]
    norm = jnp.sqrt(total)
    scale = 0.1 * (norm[0:1, 0:1] / (norm[1:2, 0:1] + 1e-06))
    n = sems.shape[0]
    rows = update_ref.shape[0] // n
    copies = []
    for at in range(n):
        span = pl.ds(at * rows, rows)
        new_weight[0, span, :] = weight_ref[0, span, :] - scale * update_ref[span, :]
        copies.append(pltpu.make_async_copy(new_weight.at[:, span], out_ref.at[:, span], sems.at[at]))
        copies[-1].start()
    for copy in copies:
        copy.wait()


def call(kernel, out_shape, *args, spaces=VMEM, out_spaces=VMEM, scratch=(), grant=40, flops=0, name=None):
    nbytes = sum(a.size * a.dtype.itemsize for a in jax.tree.leaves((args, out_shape)))
    return pl.pallas_call(
        kernel,
        out_shape=out_shape,
        in_specs=spaces if isinstance(spaces, list) else [spaces] * len(args),
        out_specs=jax.tree.map(lambda _: out_spaces, out_shape),
        scratch_shapes=scratch,
        compiler_params=pltpu.CompilerParams(vmem_limit_bytes=grant * 2**20),
        cost_estimate=pl.CostEstimate(flops=flops, bytes_accessed=nbytes, transcendentals=0),
        name=name,
    )(*args)


def tick(*arrays, flops):
    def kernel(*refs):
        refs[-1][...] = jnp.zeros(refs[-1].shape, jnp.float32)

    return call(kernel, jax.ShapeDtypeStruct((8, 128), jnp.float32), *arrays, spaces=ANY, flops=flops, name="tick")


def after(arrays, *earlier):
    return lax.optimization_barrier((arrays, earlier))[0]


def by_permutes(
    cotangent,
    route_weight,
    expert_ids,
    slot_ids,
    hidden_saved,
    down_weight,
    first_moment,
    second_moment,
):
    n_dp, owners = lax.axis_size("dp"), lax.axis_size("expert")
    n_chips = n_dp // 2
    tokens, width = cotangent.shape
    capacity, ff = hidden_saved.shape[3:]
    part = width // n_chips
    half = part // 2
    bf16, f32 = jnp.bfloat16, jnp.float32
    hidden = hidden_saved.reshape(owners * capacity, ff)

    def across(array, mask):
        return lax.ppermute(array, "dp", [(d, d ^ mask) for d in range(n_dp)])

    def along(array, shift):
        return lax.ppermute(array, "expert", [(d, (d + shift) % owners) for d in range(owners)])

    def pack(*blocks):
        size = len(blocks) * capacity
        return call(
            functools.partial(pack_kernel, owners, capacity, len(blocks)),
            [jax.ShapeDtypeStruct((size, part), bf16)] * owners,
            *blocks,
            flops=4 * 2 * size * owners * tokens * part,
            name="pack",
        )

    def multiply(columns, groups, *early, span=slice(0, ff), waits=()):
        arrays, plan = [], []

        def place(array):
            if not any(array is other for other in arrays):
                arrays.append(array)
            return [array is other for other in arrays].index(True)

        for parts, packed in groups:
            plan.append(([place(p) for p in parts], [(place(p), at, shift) for p, at, shift in packed]))
        n = columns.stop - columns.start
        return call(
            functools.partial(product_kernel, owners, capacity, columns, span.start, plan, len(early)),
            jax.ShapeDtypeStruct((n, span.stop - span.start), f32),
            *arrays,
            *early,
            *waits,
            spaces=[VMEM] * (len(arrays) + len(early)) + [ANY] * len(waits),
            flops=2 * sum(len(packed) for _, packed in plan) * capacity * n * (span.stop - span.start),
            name="product",
        )

    packed, block = jax.ShapeDtypeStruct((capacity, part), bf16), jax.ShapeDtypeStruct((tokens + TAIL, part), bf16)
    operands = cotangent, *[ids.reshape(1, tokens) for ids in (route_weight, expert_ids, slot_ids)]
    cut = call(
        functools.partial(cut_kernel, n_chips, owners, capacity),
        [packed] * owners + [block] * (n_chips - 1),
        *[pltpu.with_memory_space_constraint(array, pltpu.HBM) for array in operands],
        spaces=HBM,
        scratch=[
            pltpu.VMEM((n_chips, tokens, part), bf16),
            pltpu.VMEM((1, tokens), f32),
            pltpu.VMEM((1, tokens), jnp.int32),
            pltpu.VMEM((1, tokens), jnp.int32),
            pltpu.SemaphoreType.DMA((3 + n_chips,)),
        ],
        name="cut",
    )
    near, (to_x, to_y, to_xy) = cut[:owners], cut[owners:]
    from_x, from_y = across(to_x, 2), across(to_y, 4)
    near = [near[0]] + [along(near[shift], shift) for shift in range(1, owners)]
    mid = pack(from_y)
    mid = [mid[0], along(mid[1], 1), along(mid[2], 2), along(mid[3], 3)]
    from_xy = across(after(to_xy, from_x, from_y, near[1], near[2]), 6)
    by_x = across(after(hidden, from_x, from_y, *near), 2)
    by_y = across(after(hidden, from_x, from_y, *near), 4)
    far = pack(from_x, from_xy)
    far = [far[0]] + [along(far[shift], shift) for shift in range(1, owners)]
    left, right = after((by_x[:, : ff // 2], by_y[:, ff // 2 :]), by_x, by_y)
    by_xy = across(left, 4), across(right, 2)

    keep, give = slice(0, half), slice(half, part)
    def terms(packed, at, *shifts):
        return [(packed[shift], at, shift) for shift in shifts]

    totals = {}
    seen = tick(*mid[1:], flops=20*10**9)
    for side in (give, keep):
        groups = [((hidden,), terms(near, 0, 0, 1, 2, 3)), ((by_y,), terms(mid, 0, 0, 1, 2, 3))]
        totals[side.start] = multiply(side, groups, waits=[seen])
    seen = tick(*far[1:], *totals.values(), flops=5*10**9)
    groups = [((by_x,), terms(far, 0, 0, 1, 2, 3)), (by_xy, terms(far, 1, 0, 1, 2, 3))]
    spans = slice(0, ff // 2), slice(ff // 2, ff)
    ready = [seen, down_weight, first_moment, second_moment]
    given = [multiply(give, groups, totals[give.start], span=span, waits=ready) for span in spans]
    other = [across(part, 1) for part in given]
    kept = multiply(keep, groups, after(totals[keep.start], *given))

    state, matrix = jax.ShapeDtypeStruct((1, half, ff), f32), jax.ShapeDtypeStruct((half, ff), f32)
    grad, update, sums = call(
        update_kernel,
        [matrix, matrix, jax.ShapeDtypeStruct((8, 128), f32)],
        kept,
        *other,
        down_weight,
        first_moment,
        second_moment,
        name="update",
    )
    sums = sums + across(sums, 1)
    parts = [sums] + [across(sums, mask) for mask in (2, 4, 6)]
    new_first, new_second = call(
        moment_kernel, [state, state], after(grad, sums), first_moment, second_moment, name="moment"
    )
    new_weight = call(
        functools.partial(weight_kernel, len(parts)),
        state,
        *parts,
        down_weight,
        update,
        out_spaces=HBM,
        scratch=[pltpu.VMEM((1, half, ff), f32), pltpu.SemaphoreType.DMA((4,))],
        name="weight",
    )
    return new_weight, new_first, new_second


def solution(mesh):
    placed = (
        P(("dp", "expert"), None),
        P(("dp", "expert")),
        P(("dp", "expert")),
        P(("dp", "expert")),
        P("dp", "expert", None, None, None),
        P("expert", "dp", None),
        P("expert", "dp", None),
        P("expert", "dp", None),
    )
    return jax.shard_map(
        by_permutes if mesh.shape["dp"] == 8 else on_device,
        mesh=mesh,
        in_specs=placed,
        out_specs=(P("expert", "dp", None), P("expert", "dp", None), P("expert", "dp", None)),
        check_vma=False,
    )
```

```python
import functools

import jax
import jax.numpy as jnp
from jax import lax
from jax.experimental import pallas as pl
from jax.experimental.pallas import tpu as pltpu
from jax.sharding import PartitionSpec as P

VMEM = pl.BlockSpec(memory_space=pltpu.VMEM)
HBM = pl.BlockSpec(memory_space=pltpu.HBM)
ANY = pl.BlockSpec(memory_space=pl.ANY)
TAIL = 16
ROWS_FIRST = (((0,), (0,)), ((), ()))


def on_device(
    cotangent,
    route_weight,
    expert_ids,
    slot_ids,
    hidden_saved,
    down_weight,
    first_moment,
    second_moment,
):
    tok_rows, width = cotangent.shape
    owners = lax.axis_size("expert")
    hidden_rows = hidden_saved.reshape(-1, hidden_saved.shape[-1])
    capacity = hidden_rows.shape[0] // owners
    weight = down_weight[0]
    routed = (route_weight[:, None] * cotangent.astype(jnp.float32)).astype(jnp.bfloat16)
    target = expert_ids * capacity + slot_ids
    outgoing = jnp.zeros((owners * capacity, width), jnp.bfloat16).at[target].set(routed)
    arrived = lax.all_to_all(
        outgoing.reshape(owners, capacity, width), "expert", split_axis=0, concat_axis=0, tiled=True
    )
    arrived = arrived.reshape(owners * capacity, width)
    whole_term = lax.dot_general(
        arrived, hidden_rows, (((0,), (0,)), ((), ())), preferred_element_type=jnp.float32
    )
    grad = lax.psum_scatter(whole_term, "dp", scatter_dimension=0, tiled=True)
    new_first = 0.9 * first_moment[0] + 0.1 * grad
    new_second = 0.999 * second_moment[0] + 0.001 * grad * grad
    update = (
        new_first / (1.0 - 0.9**10) / (jnp.sqrt(new_second / (1.0 - 0.999**10)) + 1e-06)
        + 0.01 * weight
    )
    weight_sq, update_sq = lax.psum((jnp.sum(weight * weight), jnp.sum(update * update)), "dp")
    ratio = jnp.sqrt(weight_sq) / (jnp.sqrt(update_sq) + 1e-06)
    new_weight = weight - 0.1 * ratio * update
    return (new_weight[None], new_first[None], new_second[None])


def packed_rows(rows, expert_row, slot_row, expert, capacity):
    slot = lax.broadcasted_iota(jnp.int32, (capacity, rows.shape[0]), 0).astype(jnp.float32)
    place = (expert_row - expert.astype(jnp.float32)) * capacity + slot_row
    hot = jnp.where(slot == place, 1.0, 0.0).astype(jnp.bfloat16)
    return jnp.dot(hot, rows, preferred_element_type=jnp.float32).astype(jnp.bfloat16)


def cut_kernel(n_chips, owners, capacity, cot_ref, scale_ref, expert_ref, slot_ref, *refs):
    packed, blocks = refs[:owners], refs[owners : owners + n_chips - 1]
    cot, scales, experts, slots, sems = refs[owners + n_chips - 1 :]
    tokens, width = cot_ref.shape
    part = width // n_chips
    half = part // 2
    me = lax.axis_index("dp")
    chip, core = me // 2, lax.rem(me, 2)
    small = [
        pltpu.make_async_copy(src, dst, sems.at[at])
        for at, (src, dst) in enumerate([(scale_ref, scales), (expert_ref, experts), (slot_ref, slots)])
    ]
    large = []
    for mask in range(n_chips):
        columns = pl.ds(pl.multiple_of((chip ^ mask) * part, part), part)
        large.append(pltpu.make_async_copy(cot_ref.at[:, columns], cot.at[mask], sems.at[3 + mask]))
    order = (*range(1, n_chips), 0)
    for copy in small + [large[mask] for mask in order]:
        copy.start()
    for copy in small:
        copy.wait()
    scale = jnp.broadcast_to(scales[...], (128, tokens)).T
    scale = jnp.concatenate([scale] * (half // 128), axis=1)
    expert_row, slot_row = experts[...].astype(jnp.float32), slots[...].astype(jnp.float32)
    row = lax.broadcasted_iota(jnp.int32, (TAIL, tokens), 0)
    ids = jnp.where(row == 0, expert_row, jnp.where(row == 1, slot_row, 0.0)).astype(jnp.bfloat16)
    for mask in order:
        large[mask].wait()
        halves = []
        for side in range(2):
            begin = pl.multiple_of((core ^ side) * half, half)
            block = cot[mask, :, pl.ds(begin, half)].astype(jnp.float32)
            halves.append((scale * block).astype(jnp.bfloat16))
        routed = jnp.concatenate(halves, axis=1)
        if mask:
            out = blocks[mask - 1]
            out[:tokens, :] = routed
            out[tokens:, :] = jnp.concatenate([ids] * (part // tokens), axis=1)
        else:
            z = lax.axis_index("expert")
            for shift, out in enumerate(packed):
                expert = lax.rem(z + shift, owners)
                out[...] = packed_rows(routed, expert_row, slot_row, expert, capacity)


def pack_kernel(owners, capacity, n_blocks, *refs):
    z = lax.axis_index("expert")
    blocks, outs = refs[:n_blocks], refs[-owners:]
    tokens = blocks[0].shape[0] - TAIL
    for at, block in enumerate(blocks):
        ids = block[tokens:, :tokens].astype(jnp.float32)
        rows = block[:tokens, :]
        for shift, out in enumerate(outs):
            expert = lax.rem(z + shift, owners)
            out[at * capacity : (at + 1) * capacity, :] = packed_rows(rows, ids[0:1], ids[1:2], expert, capacity)


def product_kernel(owners, capacity, columns, first, plan, n_early, *refs):
    me = lax.axis_index("expert")
    used = 1 + max(max(max(parts), max(place for place, _, _ in packed)) for parts, packed in plan)
    early, out = refs[used : used + n_early], refs[-1]
    rows = [
        jnp.concatenate([refs[place][at * capacity : (at + 1) * capacity, columns] for place, at, _ in packed])
        for _, packed in plan
    ]
    wide = min(out.shape[1], *(refs[place].shape[1] for parts, _ in plan for place in parts))
    for column in range(first, first + out.shape[1], wide):
        total = None
        for left, (parts, packed) in zip(rows, plan):
            size = refs[parts[0]].shape[1]
            part = refs[parts[column // size]]
            inside = slice(column % size, column % size + wide)
            begins = [lax.rem(me + owners - shift, owners) * capacity for _, _, shift in packed]
            right = [part[pl.ds(pl.multiple_of(begin, capacity), capacity), inside] for begin in begins]
            term = lax.dot_general(left, jnp.concatenate(right), ROWS_FIRST, preferred_element_type=jnp.float32)
            total = term if total is None else total + term
        for ref in early:
            total = total + ref[:, column : column + wide]
        out[:, column - first : column - first + wide] = total


def new_moments(grad, first_ref, second_ref):
    return 0.9 * first_ref[0] + 0.1 * grad, 0.999 * second_ref[0] + 0.001 * grad * grad


def update_kernel(mine_ref, left_ref, right_ref, weight_ref, first_ref, second_ref, grad_ref, update_ref, sums):
    grad = mine_ref[...] + jnp.concatenate([left_ref[...], right_ref[...]], axis=1)
    grad_ref[...] = grad
    weight = weight_ref[0]
    first, second = new_moments(grad, first_ref, second_ref)
    first, second = first * (1.0 / (1.0 - 0.9**10)), second * (1.0 / (1.0 - 0.999**10))
    root = second * lax.rsqrt(second)
    update = first * pl.reciprocal(root + 1e-06) + 0.01 * weight
    update_ref[...] = update
    row = lax.broadcasted_iota(jnp.int32, sums.shape, 0)
    sums[...] = jnp.where(row == 0, jnp.sum(weight * weight), jnp.sum(update * update))


def moment_kernel(grad_ref, first_ref, second_ref, new_first, new_second):
    new_first[0], new_second[0] = new_moments(grad_ref[...], first_ref, second_ref)


def weight_kernel(n_sums, *refs):
    sums, (weight_ref, update_ref, out_ref, new_weight, sems) = refs[:n_sums], refs[n_sums:]
    total = sums[0][...]
    for other in sums[1:]:
        total = total + other[...]
    norm = jnp.sqrt(total)
    scale = 0.1 * (norm[0:1, 0:1] / (norm[1:2, 0:1] + 1e-06))
    n = sems.shape[0]
    rows = update_ref.shape[0] // n
    copies = []
    for at in range(n):
        span = pl.ds(at * rows, rows)
        new_weight[0, span, :] = weight_ref[0, span, :] - scale * update_ref[span, :]
        copies.append(pltpu.make_async_copy(new_weight.at[:, span], out_ref.at[:, span], sems.at[at]))
        copies[-1].start()
    for copy in copies:
        copy.wait()


def call(kernel, out_shape, *args, spaces=VMEM, out_spaces=VMEM, scratch=(), grant=40, flops=0, name=None):
    nbytes = sum(a.size * a.dtype.itemsize for a in jax.tree.leaves((args, out_shape)))
    return pl.pallas_call(
        kernel,
        out_shape=out_shape,
        in_specs=spaces if isinstance(spaces, list) else [spaces] * len(args),
        out_specs=jax.tree.map(lambda _: out_spaces, out_shape),
        scratch_shapes=scratch,
        compiler_params=pltpu.CompilerParams(vmem_limit_bytes=grant * 2**20),
        cost_estimate=pl.CostEstimate(flops=flops, bytes_accessed=nbytes, transcendentals=0),
        name=name,
    )(*args)


def tick(*arrays, flops):
    def kernel(*refs):
        refs[-1][...] = jnp.zeros(refs[-1].shape, jnp.float32)

    return call(kernel, jax.ShapeDtypeStruct((8, 128), jnp.float32), *arrays, spaces=ANY, flops=flops, name="tick")


def after(arrays, *earlier):
    return lax.optimization_barrier((arrays, earlier))[0]


def by_permutes(
    cotangent,
    route_weight,
    expert_ids,
    slot_ids,
    hidden_saved,
    down_weight,
    first_moment,
    second_moment,
):
    n_dp, owners = lax.axis_size("dp"), lax.axis_size("expert")
    n_chips = n_dp // 2
    tokens, width = cotangent.shape
    capacity, ff = hidden_saved.shape[3:]
    part = width // n_chips
    half = part // 2
    bf16, f32 = jnp.bfloat16, jnp.float32
    hidden = hidden_saved.reshape(owners * capacity, ff)

    def across(array, mask):
        return lax.ppermute(array, "dp", [(d, d ^ mask) for d in range(n_dp)])

    def along(array, shift):
        return lax.ppermute(array, "expert", [(d, (d + shift) % owners) for d in range(owners)])

    def pack(*blocks, waits=()):
        size = len(blocks) * capacity
        return call(
            functools.partial(pack_kernel, owners, capacity, len(blocks)),
            [jax.ShapeDtypeStruct((size, part), bf16)] * owners,
            *blocks,
            *waits,
            spaces=[VMEM] * len(blocks) + [ANY] * len(waits),
            flops=4 * 2 * size * owners * tokens * part,
            name="pack",
        )

    def multiply(columns, groups, *early, span=slice(0, ff), waits=()):
        arrays, plan = [], []

        def place(array):
            if not any(array is other for other in arrays):
                arrays.append(array)
            return [array is other for other in arrays].index(True)

        for parts, packed in groups:
            plan.append(([place(p) for p in parts], [(place(p), at, shift) for p, at, shift in packed]))
        n = columns.stop - columns.start
        return call(
            functools.partial(product_kernel, owners, capacity, columns, span.start, plan, len(early)),
            jax.ShapeDtypeStruct((n, span.stop - span.start), f32),
            *arrays,
            *early,
            *waits,
            spaces=[VMEM] * (len(arrays) + len(early)) + [ANY] * len(waits),
            flops=2 * sum(len(packed) for _, packed in plan) * capacity * n * (span.stop - span.start),
            name="product",
        )

    packed, block = jax.ShapeDtypeStruct((capacity, part), bf16), jax.ShapeDtypeStruct((tokens + TAIL, part), bf16)
    operands = cotangent, *[ids.reshape(1, tokens) for ids in (route_weight, expert_ids, slot_ids)]
    cut = call(
        functools.partial(cut_kernel, n_chips, owners, capacity),
        [packed] * owners + [block] * (n_chips - 1),
        *[pltpu.with_memory_space_constraint(array, pltpu.HBM) for array in operands],
        spaces=HBM,
        scratch=[
            pltpu.VMEM((n_chips, tokens, part), bf16),
            pltpu.VMEM((1, tokens), f32),
            pltpu.VMEM((1, tokens), jnp.int32),
            pltpu.VMEM((1, tokens), jnp.int32),
            pltpu.SemaphoreType.DMA((3 + n_chips,)),
        ],
        name="cut",
    )
    near, (to_x, to_y, to_xy) = cut[:owners], cut[owners:]
    from_x, from_y = across(to_x, 2), across(to_y, 4)
    near = [near[0]] + [along(near[shift], shift) for shift in range(1, owners)]
    seen = tick(near[2], flops=2*10**9)
    mid = pack(from_y, waits=[seen])
    mid = [mid[0], along(mid[1], 1), along(mid[2], 2), along(mid[3], 3)]
    late = tick(near[1], near[3], flops=2*10**9)
    from_xy = across(after(to_xy, from_x, from_y, seen), 6)
    by_x = across(after(hidden, from_x, from_y, near[2], late), 2)
    by_y = across(after(hidden, from_x, from_y, near[2], late), 4)
    far = pack(from_x, from_xy, waits=[late])
    far = [far[0]] + [along(far[shift], shift) for shift in range(1, owners)]
    left, right = after((by_x[:, : ff // 2], by_y[:, ff // 2 :]), by_x, by_y)
    by_xy = across(left, 4), across(right, 2)

    keep, give = slice(0, half), slice(half, part)
    def terms(packed, at, *shifts):
        return [(packed[shift], at, shift) for shift in shifts]

    totals = {}
    seen = tick(*mid[1:], flops=20*10**9)
    for side in (give, keep):
        groups = [((hidden,), terms(near, 0, 0, 1, 2, 3)), ((by_y,), terms(mid, 0, 0, 1, 2, 3))]
        totals[side.start] = multiply(side, groups, waits=[seen])
    seen = tick(*far[1:], *totals.values(), flops=5*10**9)
    groups = [((by_x,), terms(far, 0, 0, 1, 2, 3)), (by_xy, terms(far, 1, 0, 1, 2, 3))]
    spans = slice(0, ff // 2), slice(ff // 2, ff)
    ready = [seen, down_weight, first_moment, second_moment]
    given = [multiply(give, groups, totals[give.start], span=span, waits=ready) for span in spans]
    other = [across(part, 1) for part in given]
    kept = multiply(keep, groups, after(totals[keep.start], *given))

    state, matrix = jax.ShapeDtypeStruct((1, half, ff), f32), jax.ShapeDtypeStruct((half, ff), f32)
    grad, update, sums = call(
        update_kernel,
        [matrix, matrix, jax.ShapeDtypeStruct((8, 128), f32)],
        kept,
        *other,
        down_weight,
        first_moment,
        second_moment,
        name="update",
    )
    sums = sums + across(sums, 1)
    parts = [sums] + [across(sums, mask) for mask in (2, 4, 6)]
    new_first, new_second = call(
        moment_kernel, [state, state], after(grad, sums), first_moment, second_moment, name="moment"
    )
    new_weight = call(
        functools.partial(weight_kernel, len(parts)),
        state,
        *parts,
        down_weight,
        update,
        out_spaces=HBM,
        scratch=[pltpu.VMEM((1, half, ff), f32), pltpu.SemaphoreType.DMA((4,))],
        name="weight",
    )
    return new_weight, new_first, new_second


def solution(mesh):
    placed = (
        P(("dp", "expert"), None),
        P(("dp", "expert")),
        P(("dp", "expert")),
        P(("dp", "expert")),
        P("dp", "expert", None, None, None),
        P("expert", "dp", None),
        P("expert", "dp", None),
        P("expert", "dp", None),
    )
    return jax.shard_map(
        by_permutes if mesh.shape["dp"] == 8 else on_device,
        mesh=mesh,
        in_specs=placed,
        out_specs=(P("expert", "dp", None), P("expert", "dp", None), P("expert", "dp", None)),
        check_vma=False,
    )
```

```python
import functools

import jax
import jax.numpy as jnp
from jax import lax
from jax.experimental import pallas as pl
from jax.experimental.pallas import tpu as pltpu
from jax.sharding import PartitionSpec as P

VMEM = pl.BlockSpec(memory_space=pltpu.VMEM)
HBM = pl.BlockSpec(memory_space=pltpu.HBM)
ANY = pl.BlockSpec(memory_space=pl.ANY)
TAIL = 16
ROWS_FIRST = (((0,), (0,)), ((), ()))


def on_device(
    cotangent,
    route_weight,
    expert_ids,
    slot_ids,
    hidden_saved,
    down_weight,
    first_moment,
    second_moment,
):
    tok_rows, width = cotangent.shape
    owners = lax.axis_size("expert")
    hidden_rows = hidden_saved.reshape(-1, hidden_saved.shape[-1])
    capacity = hidden_rows.shape[0] // owners
    weight = down_weight[0]
    routed = (route_weight[:, None] * cotangent.astype(jnp.float32)).astype(jnp.bfloat16)
    target = expert_ids * capacity + slot_ids
    outgoing = jnp.zeros((owners * capacity, width), jnp.bfloat16).at[target].set(routed)
    arrived = lax.all_to_all(
        outgoing.reshape(owners, capacity, width), "expert", split_axis=0, concat_axis=0, tiled=True
    )
    arrived = arrived.reshape(owners * capacity, width)
    whole_term = lax.dot_general(
        arrived, hidden_rows, (((0,), (0,)), ((), ())), preferred_element_type=jnp.float32
    )
    grad = lax.psum_scatter(whole_term, "dp", scatter_dimension=0, tiled=True)
    new_first = 0.9 * first_moment[0] + 0.1 * grad
    new_second = 0.999 * second_moment[0] + 0.001 * grad * grad
    update = (
        new_first / (1.0 - 0.9**10) / (jnp.sqrt(new_second / (1.0 - 0.999**10)) + 1e-06)
        + 0.01 * weight
    )
    weight_sq, update_sq = lax.psum((jnp.sum(weight * weight), jnp.sum(update * update)), "dp")
    ratio = jnp.sqrt(weight_sq) / (jnp.sqrt(update_sq) + 1e-06)
    new_weight = weight - 0.1 * ratio * update
    return (new_weight[None], new_first[None], new_second[None])


def packed_rows(rows, expert_row, slot_row, expert, capacity):
    slot = lax.broadcasted_iota(jnp.int32, (capacity, rows.shape[0]), 0).astype(jnp.float32)
    place = (expert_row - expert.astype(jnp.float32)) * capacity + slot_row
    hot = jnp.where(slot == place, 1.0, 0.0).astype(jnp.bfloat16)
    return jnp.dot(hot, rows, preferred_element_type=jnp.float32).astype(jnp.bfloat16)


def cut_kernel(n_chips, owners, capacity, cot_ref, scale_ref, expert_ref, slot_ref, *refs):
    packed, blocks = refs[:owners], refs[owners : owners + n_chips - 1]
    cot, scales, experts, slots, sems = refs[owners + n_chips - 1 :]
    tokens, width = cot_ref.shape
    part = width // n_chips
    half = part // 2
    me = lax.axis_index("dp")
    chip, core = me // 2, lax.rem(me, 2)
    small = [
        pltpu.make_async_copy(src, dst, sems.at[at])
        for at, (src, dst) in enumerate([(scale_ref, scales), (expert_ref, experts), (slot_ref, slots)])
    ]
    large = []
    for mask in range(n_chips):
        columns = pl.ds(pl.multiple_of((chip ^ mask) * part, part), part)
        large.append(pltpu.make_async_copy(cot_ref.at[:, columns], cot.at[mask], sems.at[3 + mask]))
    order = (*range(1, n_chips), 0)
    for copy in small + [large[mask] for mask in order]:
        copy.start()
    for copy in small:
        copy.wait()
    scale = jnp.broadcast_to(scales[...], (128, tokens)).T
    scale = jnp.concatenate([scale] * (half // 128), axis=1)
    expert_row, slot_row = experts[...].astype(jnp.float32), slots[...].astype(jnp.float32)
    row = lax.broadcasted_iota(jnp.int32, (TAIL, tokens), 0)
    ids = jnp.where(row == 0, expert_row, jnp.where(row == 1, slot_row, 0.0)).astype(jnp.bfloat16)
    for mask in order:
        large[mask].wait()
        halves = []
        for side in range(2):
            begin = pl.multiple_of((core ^ side) * half, half)
            block = cot[mask, :, pl.ds(begin, half)].astype(jnp.float32)
            halves.append((scale * block).astype(jnp.bfloat16))
        routed = jnp.concatenate(halves, axis=1)
        if mask:
            out = blocks[mask - 1]
            out[:tokens, :] = routed
            out[tokens:, :] = jnp.concatenate([ids] * (part // tokens), axis=1)
        else:
            z = lax.axis_index("expert")
            for shift, out in enumerate(packed):
                expert = lax.rem(z + shift, owners)
                out[...] = packed_rows(routed, expert_row, slot_row, expert, capacity)


def pack_kernel(owners, capacity, n_blocks, *refs):
    z = lax.axis_index("expert")
    blocks, outs = refs[:n_blocks], refs[-owners:]
    tokens = blocks[0].shape[0] - TAIL
    for at, block in enumerate(blocks):
        ids = block[tokens:, :tokens].astype(jnp.float32)
        rows = block[:tokens, :]
        for shift, out in enumerate(outs):
            expert = lax.rem(z + shift, owners)
            out[at * capacity : (at + 1) * capacity, :] = packed_rows(rows, ids[0:1], ids[1:2], expert, capacity)


def product_kernel(owners, capacity, columns, first, plan, n_early, *refs):
    me = lax.axis_index("expert")
    used = 1 + max(max(max(parts), max(place for place, _, _ in packed)) for parts, packed in plan)
    early, out = refs[used : used + n_early], refs[-1]
    rows = [
        jnp.concatenate([refs[place][at * capacity : (at + 1) * capacity, columns] for place, at, _ in packed])
        for _, packed in plan
    ]
    wide = min(out.shape[1], *(refs[place].shape[1] for parts, _ in plan for place in parts))
    for column in range(first, first + out.shape[1], wide):
        total = None
        for left, (parts, packed) in zip(rows, plan):
            size = refs[parts[0]].shape[1]
            part = refs[parts[column // size]]
            inside = slice(column % size, column % size + wide)
            begins = [lax.rem(me + owners - shift, owners) * capacity for _, _, shift in packed]
            right = [part[pl.ds(pl.multiple_of(begin, capacity), capacity), inside] for begin in begins]
            term = lax.dot_general(left, jnp.concatenate(right), ROWS_FIRST, preferred_element_type=jnp.float32)
            total = term if total is None else total + term
        for ref in early:
            total = total + ref[:, column : column + wide]
        out[:, column - first : column - first + wide] = total


def new_moments(grad, first, second):
    return 0.9 * first + 0.1 * grad, 0.999 * second + 0.001 * grad * grad


def update_kernel(begin, mine_ref, other_ref, weight_ref, first_ref, second_ref, *refs):
    earlier, (grad_ref, update_ref, sums) = refs[:-3], refs[-3:]
    columns = slice(begin, begin + other_ref.shape[1])
    grad = mine_ref[:, columns] + other_ref[...]
    grad_ref[...] = grad
    weight = weight_ref[0, :, columns]
    first, second = new_moments(grad, first_ref[0, :, columns], second_ref[0, :, columns])
    first, second = first * (1.0 / (1.0 - 0.9**10)), second * (1.0 / (1.0 - 0.999**10))
    root = second * lax.rsqrt(second)
    update = first * pl.reciprocal(root + 1e-06) + 0.01 * weight
    update_ref[...] = update
    row = lax.broadcasted_iota(jnp.int32, sums.shape, 0)
    total = jnp.where(row == 0, jnp.sum(weight * weight), jnp.sum(update * update))
    for ref in earlier:
        total = total + ref[...]
    sums[...] = total


def moment_kernel(left_ref, right_ref, first_ref, second_ref, new_first, new_second):
    begin = 0
    for grad_ref in (left_ref, right_ref):
        columns = slice(begin, begin + grad_ref.shape[1])
        first, second = new_moments(grad_ref[...], first_ref[0, :, columns], second_ref[0, :, columns])
        new_first[0, :, columns], new_second[0, :, columns] = first, second
        begin += grad_ref.shape[1]


def weight_kernel(n_sums, *refs):
    sums, (weight_ref, left_ref, right_ref, out_ref, new_weight, sems) = refs[:n_sums], refs[n_sums:]
    total = sums[0][...]
    for other in sums[1:]:
        total = total + other[...]
    norm = jnp.sqrt(total)
    scale = 0.1 * (norm[0:1, 0:1] / (norm[1:2, 0:1] + 1e-06))
    n = sems.shape[0]
    rows = left_ref.shape[0] // n
    copies = []
    for at in range(n):
        span = pl.ds(at * rows, rows)
        update = jnp.concatenate([left_ref[span, :], right_ref[span, :]], axis=1)
        new_weight[0, span, :] = weight_ref[0, span, :] - scale * update
        copies.append(pltpu.make_async_copy(new_weight.at[:, span], out_ref.at[:, span], sems.at[at]))
        copies[-1].start()
    for copy in copies:
        copy.wait()


def call(kernel, out_shape, *args, spaces=VMEM, out_spaces=VMEM, scratch=(), grant=40, flops=0, name=None):
    nbytes = sum(a.size * a.dtype.itemsize for a in jax.tree.leaves((args, out_shape)))
    return pl.pallas_call(
        kernel,
        out_shape=out_shape,
        in_specs=spaces if isinstance(spaces, list) else [spaces] * len(args),
        out_specs=jax.tree.map(lambda _: out_spaces, out_shape),
        scratch_shapes=scratch,
        compiler_params=pltpu.CompilerParams(vmem_limit_bytes=grant * 2**20),
        cost_estimate=pl.CostEstimate(flops=flops, bytes_accessed=nbytes, transcendentals=0),
        name=name,
    )(*args)


def tick(*arrays, flops):
    def kernel(*refs):
        refs[-1][...] = jnp.zeros(refs[-1].shape, jnp.float32)

    return call(kernel, jax.ShapeDtypeStruct((8, 128), jnp.float32), *arrays, spaces=ANY, flops=flops, name="tick")


def after(arrays, *earlier):
    return lax.optimization_barrier((arrays, earlier))[0]


def by_permutes(
    cotangent,
    route_weight,
    expert_ids,
    slot_ids,
    hidden_saved,
    down_weight,
    first_moment,
    second_moment,
):
    n_dp, owners = lax.axis_size("dp"), lax.axis_size("expert")
    n_chips = n_dp // 2
    tokens, width = cotangent.shape
    capacity, ff = hidden_saved.shape[3:]
    part = width // n_chips
    half = part // 2
    bf16, f32 = jnp.bfloat16, jnp.float32
    hidden = hidden_saved.reshape(owners * capacity, ff)

    def across(array, mask):
        return lax.ppermute(array, "dp", [(d, d ^ mask) for d in range(n_dp)])

    def along(array, shift):
        return lax.ppermute(array, "expert", [(d, (d + shift) % owners) for d in range(owners)])

    def pack(*blocks, waits=()):
        size = len(blocks) * capacity
        return call(
            functools.partial(pack_kernel, owners, capacity, len(blocks)),
            [jax.ShapeDtypeStruct((size, part), bf16)] * owners,
            *blocks,
            *waits,
            spaces=[VMEM] * len(blocks) + [ANY] * len(waits),
            flops=4 * 2 * size * owners * tokens * part,
            name="pack",
        )

    def multiply(columns, groups, *early, span=slice(0, ff), waits=()):
        arrays, plan = [], []

        def place(array):
            if not any(array is other for other in arrays):
                arrays.append(array)
            return [array is other for other in arrays].index(True)

        for parts, packed in groups:
            plan.append(([place(p) for p in parts], [(place(p), at, shift) for p, at, shift in packed]))
        n = columns.stop - columns.start
        return call(
            functools.partial(product_kernel, owners, capacity, columns, span.start, plan, len(early)),
            jax.ShapeDtypeStruct((n, span.stop - span.start), f32),
            *arrays,
            *early,
            *waits,
            spaces=[VMEM] * (len(arrays) + len(early)) + [ANY] * len(waits),
            flops=2 * sum(len(packed) for _, packed in plan) * capacity * n * (span.stop - span.start),
            name="product",
        )

    packed, block = jax.ShapeDtypeStruct((capacity, part), bf16), jax.ShapeDtypeStruct((tokens + TAIL, part), bf16)
    operands = cotangent, *[ids.reshape(1, tokens) for ids in (route_weight, expert_ids, slot_ids)]
    cut = call(
        functools.partial(cut_kernel, n_chips, owners, capacity),
        [packed] * owners + [block] * (n_chips - 1),
        *[pltpu.with_memory_space_constraint(array, pltpu.HBM) for array in operands],
        spaces=HBM,
        scratch=[
            pltpu.VMEM((n_chips, tokens, part), bf16),
            pltpu.VMEM((1, tokens), f32),
            pltpu.VMEM((1, tokens), jnp.int32),
            pltpu.VMEM((1, tokens), jnp.int32),
            pltpu.SemaphoreType.DMA((3 + n_chips,)),
        ],
        name="cut",
    )
    near, (to_x, to_y, to_xy) = cut[:owners], cut[owners:]
    from_x, from_y = across(to_x, 2), across(to_y, 4)
    near = [near[0]] + [along(near[shift], shift) for shift in range(1, owners)]
    seen = tick(near[2], flops=2*10**9)
    mid = pack(from_y, waits=[seen])
    mid = [mid[0], along(mid[1], 1), along(mid[2], 2), along(mid[3], 3)]
    late = tick(near[1], near[3], flops=2*10**9)
    from_xy = across(after(to_xy, from_x, from_y, seen), 6)
    by_x = across(after(hidden, from_x, from_y, near[2], late), 2)
    by_y = across(after(hidden, from_x, from_y, near[2], late), 4)
    far = pack(from_x, from_xy, waits=[late])
    far = [far[0]] + [along(far[shift], shift) for shift in range(1, owners)]
    left, right = after((by_x[:, : ff // 2], by_y[:, ff // 2 :]), by_x, by_y)
    by_xy = across(left, 4), across(right, 2)

    keep, give = slice(0, half), slice(half, part)
    def terms(packed, at, *shifts):
        return [(packed[shift], at, shift) for shift in shifts]

    totals = {}
    seen = tick(*mid[1:], flops=20*10**9)
    for side in (give, keep):
        groups = [((hidden,), terms(near, 0, 0, 1, 2, 3)), ((by_y,), terms(mid, 0, 0, 1, 2, 3))]
        totals[side.start] = multiply(side, groups, waits=[seen])
    seen = tick(far[1], far[2], *totals.values(), flops=5*10**9)
    state_in = down_weight, first_moment, second_moment
    for side in (give, keep):
        groups = [((by_x,), terms(far, 0, 0, 1, 2)), (by_xy, terms(far, 1, 0, 1, 2))]
        totals[side.start] = multiply(side, groups, totals[side.start], waits=[seen, *state_in])
    seen = tick(far[3], *totals.values(), flops=5*10**9)
    groups = [((by_x,), terms(far, 0, 3)), (by_xy, terms(far, 1, 3))]
    spans = slice(0, ff // 2), slice(ff // 2, ff)
    ready = [seen]
    given = [multiply(give, groups, totals[give.start], span=span, waits=ready) for span in spans]
    other = [across(part, 1) for part in given]
    kept = multiply(keep, groups, after(totals[keep.start], *given))

    state = jax.ShapeDtypeStruct((1, half, ff), f32)
    grads, updates, sums = [], [], []
    for span, part in zip(spans, other):
        piece = jax.ShapeDtypeStruct(part.shape, f32)
        grad, update, total = call(
            functools.partial(update_kernel, span.start),
            [piece, piece, jax.ShapeDtypeStruct((8, 128), f32)],
            kept,
            part,
            *state_in,
            *sums,
            name="update",
        )
        grads, updates, sums = [*grads, grad], [*updates, update], [total]
    sums = sums[0] + across(sums[0], 1)
    parts = [sums] + [across(sums, mask) for mask in (2, 4, 6)]
    new_first, new_second = call(
        moment_kernel, [state, state], *after(tuple(grads), sums), first_moment, second_moment, name="moment"
    )
    new_weight = call(
        functools.partial(weight_kernel, len(parts)),
        state,
        *parts,
        down_weight,
        *updates,
        out_spaces=HBM,
        scratch=[pltpu.VMEM((1, half, ff), f32), pltpu.SemaphoreType.DMA((4,))],
        name="weight",
    )
    return new_weight, new_first, new_second


def solution(mesh):
    placed = (
        P(("dp", "expert"), None),
        P(("dp", "expert")),
        P(("dp", "expert")),
        P(("dp", "expert")),
        P("dp", "expert", None, None, None),
        P("expert", "dp", None),
        P("expert", "dp", None),
        P("expert", "dp", None),
    )
    return jax.shard_map(
        by_permutes if mesh.shape["dp"] == 8 else on_device,
        mesh=mesh,
        in_specs=placed,
        out_specs=(P("expert", "dp", None), P("expert", "dp", None), P("expert", "dp", None)),
        check_vma=False,
    )
```

```python
import functools

import jax
import jax.numpy as jnp
from jax import lax
from jax.experimental import pallas as pl
from jax.experimental.pallas import tpu as pltpu
from jax.sharding import PartitionSpec as P

VMEM = pl.BlockSpec(memory_space=pltpu.VMEM)
HBM = pl.BlockSpec(memory_space=pltpu.HBM)
ANY = pl.BlockSpec(memory_space=pl.ANY)
TAIL = 16
ROWS_FIRST = (((0,), (0,)), ((), ()))
UNIT = 10**9


def on_device(
    cotangent,
    route_weight,
    expert_ids,
    slot_ids,
    hidden_saved,
    down_weight,
    first_moment,
    second_moment,
):
    tok_rows, width = cotangent.shape
    owners = lax.axis_size("expert")
    hidden_rows = hidden_saved.reshape(-1, hidden_saved.shape[-1])
    capacity = hidden_rows.shape[0] // owners
    weight = down_weight[0]
    routed = (route_weight[:, None] * cotangent.astype(jnp.float32)).astype(jnp.bfloat16)
    target = expert_ids * capacity + slot_ids
    outgoing = jnp.zeros((owners * capacity, width), jnp.bfloat16).at[target].set(routed)
    arrived = lax.all_to_all(
        outgoing.reshape(owners, capacity, width), "expert", split_axis=0, concat_axis=0, tiled=True
    )
    arrived = arrived.reshape(owners * capacity, width)
    whole_term = lax.dot_general(
        arrived, hidden_rows, (((0,), (0,)), ((), ())), preferred_element_type=jnp.float32
    )
    grad = lax.psum_scatter(whole_term, "dp", scatter_dimension=0, tiled=True)
    new_first = 0.9 * first_moment[0] + 0.1 * grad
    new_second = 0.999 * second_moment[0] + 0.001 * grad * grad
    update = (
        new_first / (1.0 - 0.9**10) / (jnp.sqrt(new_second / (1.0 - 0.999**10)) + 1e-06)
        + 0.01 * weight
    )
    weight_sq, update_sq = lax.psum((jnp.sum(weight * weight), jnp.sum(update * update)), "dp")
    ratio = jnp.sqrt(weight_sq) / (jnp.sqrt(update_sq) + 1e-06)
    new_weight = weight - 0.1 * ratio * update
    return (new_weight[None], new_first[None], new_second[None])


def packed_rows(rows, expert_row, slot_row, expert, capacity):
    slot = lax.broadcasted_iota(jnp.int32, (capacity, rows.shape[0]), 0).astype(jnp.float32)
    place = (expert_row - expert.astype(jnp.float32)) * capacity + slot_row
    hot = jnp.where(slot == place, 1.0, 0.0).astype(jnp.bfloat16)
    return jnp.dot(hot, rows, preferred_element_type=jnp.float32).astype(jnp.bfloat16)


def cut_kernel(n_chips, owners, capacity, cot_ref, scale_ref, expert_ref, slot_ref, *refs):
    packed, blocks = refs[:owners], refs[owners : owners + n_chips - 1]
    cot, scales, experts, slots, sems = refs[owners + n_chips - 1 :]
    tokens, width = cot_ref.shape
    part = width // n_chips
    half = part // 2
    me = lax.axis_index("dp")
    chip, core = me // 2, lax.rem(me, 2)
    small = [
        pltpu.make_async_copy(src, dst, sems.at[at])
        for at, (src, dst) in enumerate([(scale_ref, scales), (expert_ref, experts), (slot_ref, slots)])
    ]
    large = []
    for mask in range(n_chips):
        columns = pl.ds(pl.multiple_of((chip ^ mask) * part, part), part)
        large.append(pltpu.make_async_copy(cot_ref.at[:, columns], cot.at[mask], sems.at[3 + mask]))
    order = (*range(1, n_chips), 0)
    for copy in small + [large[mask] for mask in order]:
        copy.start()
    for copy in small:
        copy.wait()
    scale = jnp.broadcast_to(scales[...], (128, tokens)).T
    scale = jnp.concatenate([scale] * (half // 128), axis=1)
    expert_row, slot_row = experts[...].astype(jnp.float32), slots[...].astype(jnp.float32)
    row = lax.broadcasted_iota(jnp.int32, (TAIL, tokens), 0)
    ids = jnp.where(row == 0, expert_row, jnp.where(row == 1, slot_row, 0.0)).astype(jnp.bfloat16)
    for mask in order:
        large[mask].wait()
        halves = []
        for side in range(2):
            begin = pl.multiple_of((core ^ side) * half, half)
            block = cot[mask, :, pl.ds(begin, half)].astype(jnp.float32)
            halves.append((scale * block).astype(jnp.bfloat16))
        routed = jnp.concatenate(halves, axis=1)
        if mask:
            out = blocks[mask - 1]
            out[:tokens, :] = routed
            out[tokens:, :] = jnp.concatenate([ids] * (part // tokens), axis=1)
        else:
            z = lax.axis_index("expert")
            for shift, out in enumerate(packed):
                expert = lax.rem(z + shift, owners)
                out[...] = packed_rows(routed, expert_row, slot_row, expert, capacity)


def pack_kernel(owners, capacity, n_blocks, *refs):
    z = lax.axis_index("expert")
    blocks, outs = refs[:n_blocks], refs[-owners:]
    tokens = blocks[0].shape[0] - TAIL
    for at, block in enumerate(blocks):
        ids = block[tokens:, :tokens].astype(jnp.float32)
        rows = block[:tokens, :]
        for shift, out in enumerate(outs):
            expert = lax.rem(z + shift, owners)
            out[at * capacity : (at + 1) * capacity, :] = packed_rows(rows, ids[0:1], ids[1:2], expert, capacity)


def product_kernel(owners, capacity, columns, first, plan, n_early, *refs):
    me = lax.axis_index("expert")
    used = 1 + max(max(max(parts), max(place for place, _, _ in packed)) for parts, packed in plan)
    early, out = refs[used : used + n_early], refs[-1]
    rows = [
        jnp.concatenate([refs[place][at * capacity : (at + 1) * capacity, columns] for place, at, _ in packed])
        for _, packed in plan
    ]
    wide = min(out.shape[1], *(refs[place].shape[1] for parts, _ in plan for place in parts))
    for column in range(first, first + out.shape[1], wide):
        total = None
        for left, (parts, packed) in zip(rows, plan):
            size = refs[parts[0]].shape[1]
            part = refs[parts[column // size]]
            inside = slice(column % size, column % size + wide)
            begins = [lax.rem(me + owners - shift, owners) * capacity for _, _, shift in packed]
            right = [part[pl.ds(pl.multiple_of(begin, capacity), capacity), inside] for begin in begins]
            term = lax.dot_general(left, jnp.concatenate(right), ROWS_FIRST, preferred_element_type=jnp.float32)
            total = term if total is None else total + term
        for ref in early:
            total = total + ref[:, column : column + wide]
        out[:, column - first : column - first + wide] = total


def new_moments(grad, first, second):
    return 0.9 * first + 0.1 * grad, 0.999 * second + 0.001 * grad * grad


def update_kernel(begin, mine_ref, other_ref, weight_ref, first_ref, second_ref, *refs):
    earlier, (grad_ref, update_ref, sums) = refs[:-3], refs[-3:]
    columns = slice(begin, begin + other_ref.shape[1])
    grad = mine_ref[:, columns] + other_ref[...]
    grad_ref[...] = grad
    weight = weight_ref[0, :, columns]
    first, second = new_moments(grad, first_ref[0, :, columns], second_ref[0, :, columns])
    first, second = first * (1.0 / (1.0 - 0.9**10)), second * (1.0 / (1.0 - 0.999**10))
    root = second * lax.rsqrt(second)
    update = first * pl.reciprocal(root + 1e-06) + 0.01 * weight
    update_ref[...] = update
    row = lax.broadcasted_iota(jnp.int32, sums.shape, 0)
    total = jnp.where(row == 0, jnp.sum(weight * weight), jnp.sum(update * update))
    for ref in earlier:
        total = total + ref[...]
    sums[...] = total


def moment_kernel(left_ref, right_ref, first_ref, second_ref, new_first, new_second):
    begin = 0
    for grad_ref in (left_ref, right_ref):
        columns = slice(begin, begin + grad_ref.shape[1])
        first, second = new_moments(grad_ref[...], first_ref[0, :, columns], second_ref[0, :, columns])
        new_first[0, :, columns], new_second[0, :, columns] = first, second
        begin += grad_ref.shape[1]


def weight_kernel(n_sums, *refs):
    sums, (weight_ref, left_ref, right_ref, out_ref, new_weight, sems) = refs[:n_sums], refs[n_sums:]
    total = sums[0][...]
    for other in sums[1:]:
        total = total + other[...]
    norm = jnp.sqrt(total)
    scale = 0.1 * (norm[0:1, 0:1] / (norm[1:2, 0:1] + 1e-06))
    n = sems.shape[0]
    rows = left_ref.shape[0] // n
    copies = []
    for at in range(n):
        span = pl.ds(at * rows, rows)
        update = jnp.concatenate([left_ref[span, :], right_ref[span, :]], axis=1)
        new_weight[0, span, :] = weight_ref[0, span, :] - scale * update
        copies.append(pltpu.make_async_copy(new_weight.at[:, span], out_ref.at[:, span], sems.at[at]))
        copies[-1].start()
    for copy in copies:
        copy.wait()


def call(kernel, out_shape, *args, spaces=VMEM, out_spaces=VMEM, scratch=(), flops=0, name=None):
    nbytes = sum(a.size * a.dtype.itemsize for a in jax.tree.leaves((args, out_shape)))
    return pl.pallas_call(
        kernel,
        out_shape=out_shape,
        in_specs=spaces if isinstance(spaces, list) else [spaces] * len(args),
        out_specs=jax.tree.map(lambda _: out_spaces, out_shape),
        scratch_shapes=scratch,
        compiler_params=pltpu.CompilerParams(vmem_limit_bytes=40 * 2**20),
        cost_estimate=pl.CostEstimate(flops=flops, bytes_accessed=nbytes, transcendentals=0),
        name=name,
    )(*args)


def tick(*arrays, flops):
    def kernel(*refs):
        refs[-1][...] = jnp.zeros(refs[-1].shape, jnp.float32)

    return call(kernel, jax.ShapeDtypeStruct((8, 128), jnp.float32), *arrays, spaces=ANY, flops=flops, name="tick")


def after(arrays, *earlier):
    return lax.optimization_barrier((arrays, earlier))[0]


def by_permutes(
    cotangent,
    route_weight,
    expert_ids,
    slot_ids,
    hidden_saved,
    down_weight,
    first_moment,
    second_moment,
):
    n_dp, owners = lax.axis_size("dp"), lax.axis_size("expert")
    n_chips = n_dp // 2
    tokens, width = cotangent.shape
    capacity, ff = hidden_saved.shape[3:]
    part = width // n_chips
    half = part // 2
    bf16, f32 = jnp.bfloat16, jnp.float32
    hidden = hidden_saved.reshape(owners * capacity, ff)

    def across(array, mask):
        return lax.ppermute(array, "dp", [(d, d ^ mask) for d in range(n_dp)])

    def along(array, shift):
        return lax.ppermute(array, "expert", [(d, (d + shift) % owners) for d in range(owners)])

    def pack(*blocks, waits=()):
        size = len(blocks) * capacity
        return call(
            functools.partial(pack_kernel, owners, capacity, len(blocks)),
            [jax.ShapeDtypeStruct((size, part), bf16)] * owners,
            *blocks,
            *waits,
            spaces=[VMEM] * len(blocks) + [ANY] * len(waits),
            flops=4 * 2 * size * owners * tokens * part,
            name="pack",
        )

    def multiply(columns, groups, *early, span=slice(0, ff), waits=()):
        arrays, plan = [], []

        def place(array):
            if not any(array is other for other in arrays):
                arrays.append(array)
            return [array is other for other in arrays].index(True)

        for parts, packed in groups:
            plan.append(([place(p) for p in parts], [(place(p), at, shift) for p, at, shift in packed]))
        n = columns.stop - columns.start
        return call(
            functools.partial(product_kernel, owners, capacity, columns, span.start, plan, len(early)),
            jax.ShapeDtypeStruct((n, span.stop - span.start), f32),
            *arrays,
            *early,
            *waits,
            spaces=[VMEM] * (len(arrays) + len(early)) + [ANY] * len(waits),
            flops=2 * sum(len(packed) for _, packed in plan) * capacity * n * (span.stop - span.start),
            name="product",
        )

    packed, block = jax.ShapeDtypeStruct((capacity, part), bf16), jax.ShapeDtypeStruct((tokens + TAIL, part), bf16)
    operands = cotangent, *[ids.reshape(1, tokens) for ids in (route_weight, expert_ids, slot_ids)]
    cut = call(
        functools.partial(cut_kernel, n_chips, owners, capacity),
        [packed] * owners + [block] * (n_chips - 1),
        *[pltpu.with_memory_space_constraint(array, pltpu.HBM) for array in operands],
        spaces=HBM,
        scratch=[
            pltpu.VMEM((n_chips, tokens, part), bf16),
            pltpu.VMEM((1, tokens), f32),
            pltpu.VMEM((1, tokens), jnp.int32),
            pltpu.VMEM((1, tokens), jnp.int32),
            pltpu.SemaphoreType.DMA((3 + n_chips,)),
        ],
        name="cut",
    )
    near, (to_x, to_y, to_xy) = cut[:owners], cut[owners:]
    from_x, from_y = across(to_x, 2), across(to_y, 4)
    near = [near[0]] + [along(near[shift], shift) for shift in range(1, owners)]
    seen = tick(near[2], flops=2 * UNIT)
    mid = pack(from_x, waits=[seen])
    mid = [mid[0]] + [along(mid[shift], shift) for shift in range(1, owners)]
    late = tick(near[1], near[3], flops=2 * UNIT)
    from_xy = across(after(to_xy, from_x, from_y, seen), 6)
    far = pack(from_y, from_xy, waits=[late])
    far = [far[0]] + [along(far[shift], shift) for shift in range(1, owners)]
    sent = after(hidden, from_x, from_y, near[2], late)
    by_x, by_y = across(sent, 2), across(sent, 4)
    by_xy = across(by_x[:, : ff // 2], 4), across(by_y[:, ff // 2 :], 2)

    def terms(packed, at, *shifts):
        return [(packed[shift], at, shift) for shift in shifts]

    keep, give = slice(0, half), slice(half, part)
    spans = slice(0, ff // 2), slice(ff // 2, ff)
    state_in = down_weight, first_moment, second_moment
    seen = tick(*mid[1:], flops=20 * UNIT)
    groups = [((hidden,), terms(near, 0, 0, 1, 2, 3)), ((by_x,), terms(mid, 0, 0, 1, 2, 3))]
    total = {side: multiply(side, groups, waits=[seen]) for side in (give, keep)}
    seen = tick(far[1], far[2], *total.values(), flops=5 * UNIT)
    groups = [((by_y,), terms(far, 0, 0, 1, 2)), (by_xy, terms(far, 1, 0, 1, 2))]
    total = {side: multiply(side, groups, early, waits=[seen, *state_in]) for side, early in total.items()}
    seen = tick(far[3], *total.values(), flops=5 * UNIT)
    groups = [((by_y,), terms(far, 0, 3)), (by_xy, terms(far, 1, 3))]
    given = [multiply(give, groups, total[give], span=span, waits=[seen]) for span in spans]
    other = [across(part, 1) for part in given]
    kept = multiply(keep, groups, after(total[keep], *given))

    state = jax.ShapeDtypeStruct((1, half, ff), f32)
    grads, updates, sums = [], [], []
    for span, part in zip(spans, other):
        piece = jax.ShapeDtypeStruct(part.shape, f32)
        grad, update, total = call(
            functools.partial(update_kernel, span.start),
            [piece, piece, jax.ShapeDtypeStruct((8, 128), f32)],
            kept,
            part,
            *state_in,
            *sums,
            name="update",
        )
        grads, updates, sums = [*grads, grad], [*updates, update], [total]
    sums = sums[0] + across(sums[0], 1)
    parts = [sums] + [across(sums, mask) for mask in (2, 4, 6)]
    new_first, new_second = call(
        moment_kernel, [state, state], *after(tuple(grads), sums), first_moment, second_moment, name="moment"
    )
    new_weight = call(
        functools.partial(weight_kernel, len(parts)),
        state,
        *parts,
        down_weight,
        *updates,
        out_spaces=HBM,
        scratch=[pltpu.VMEM((1, half, ff), f32), pltpu.SemaphoreType.DMA((4,))],
        name="weight",
    )
    return new_weight, new_first, new_second


def solution(mesh):
    placed = (
        P(("dp", "expert"), None),
        P(("dp", "expert")),
        P(("dp", "expert")),
        P(("dp", "expert")),
        P("dp", "expert", None, None, None),
        P("expert", "dp", None),
        P("expert", "dp", None),
        P("expert", "dp", None),
    )
    return jax.shard_map(
        by_permutes if (mesh.shape["dp"], mesh.shape["expert"]) == (8, 4) else on_device,
        mesh=mesh,
        in_specs=placed,
        out_specs=(P("expert", "dp", None), P("expert", "dp", None), P("expert", "dp", None)),
        check_vma=False,
    )
```

```python
import functools

import jax
import jax.numpy as jnp
from jax import lax
from jax.experimental import pallas as pl
from jax.experimental.pallas import tpu as pltpu
from jax.sharding import PartitionSpec as P

VMEM = pl.BlockSpec(memory_space=pltpu.VMEM)
HBM = pl.BlockSpec(memory_space=pltpu.HBM)
ANY = pl.BlockSpec(memory_space=pl.ANY)
TAIL = 16
ROWS_FIRST = (((0,), (0,)), ((), ()))
UNIT = 10**9


def on_device(
    cotangent,
    route_weight,
    expert_ids,
    slot_ids,
    hidden_saved,
    down_weight,
    first_moment,
    second_moment,
):
    tok_rows, width = cotangent.shape
    owners = lax.axis_size("expert")
    hidden_rows = hidden_saved.reshape(-1, hidden_saved.shape[-1])
    capacity = hidden_rows.shape[0] // owners
    weight = down_weight[0]
    routed = (route_weight[:, None] * cotangent.astype(jnp.float32)).astype(jnp.bfloat16)
    target = expert_ids * capacity + slot_ids
    outgoing = jnp.zeros((owners * capacity, width), jnp.bfloat16).at[target].set(routed)
    arrived = lax.all_to_all(
        outgoing.reshape(owners, capacity, width), "expert", split_axis=0, concat_axis=0, tiled=True
    )
    arrived = arrived.reshape(owners * capacity, width)
    whole_term = lax.dot_general(
        arrived, hidden_rows, (((0,), (0,)), ((), ())), preferred_element_type=jnp.float32
    )
    grad = lax.psum_scatter(whole_term, "dp", scatter_dimension=0, tiled=True)
    new_first = 0.9 * first_moment[0] + 0.1 * grad
    new_second = 0.999 * second_moment[0] + 0.001 * grad * grad
    update = (
        new_first / (1.0 - 0.9**10) / (jnp.sqrt(new_second / (1.0 - 0.999**10)) + 1e-06)
        + 0.01 * weight
    )
    weight_sq, update_sq = lax.psum((jnp.sum(weight * weight), jnp.sum(update * update)), "dp")
    ratio = jnp.sqrt(weight_sq) / (jnp.sqrt(update_sq) + 1e-06)
    new_weight = weight - 0.1 * ratio * update
    return (new_weight[None], new_first[None], new_second[None])


def packed_rows(rows, expert_row, slot_row, expert, capacity):
    slot = lax.broadcasted_iota(jnp.int32, (capacity, rows.shape[0]), 0).astype(jnp.float32)
    place = (expert_row - expert.astype(jnp.float32)) * capacity + slot_row
    hot = jnp.where(slot == place, 1.0, 0.0).astype(jnp.bfloat16)
    return jnp.dot(hot, rows, preferred_element_type=jnp.float32).astype(jnp.bfloat16)


def cut_kernel(n_chips, owners, capacity, cot_ref, scale_ref, expert_ref, slot_ref, *refs):
    packed, blocks = refs[:owners], refs[owners : owners + n_chips - 1]
    cot, scales, experts, slots, sems = refs[owners + n_chips - 1 :]
    tokens, width = cot_ref.shape
    part = width // n_chips
    half = part // 2
    me = lax.axis_index("dp")
    chip, core = me // 2, lax.rem(me, 2)
    small = [
        pltpu.make_async_copy(src, dst, sems.at[at])
        for at, (src, dst) in enumerate([(scale_ref, scales), (expert_ref, experts), (slot_ref, slots)])
    ]
    large = []
    for mask in range(n_chips):
        columns = pl.ds(pl.multiple_of((chip ^ mask) * part, part), part)
        large.append(pltpu.make_async_copy(cot_ref.at[:, columns], cot.at[mask], sems.at[3 + mask]))
    order = (*range(1, n_chips), 0)
    for copy in small + [large[mask] for mask in order]:
        copy.start()
    for copy in small:
        copy.wait()
    scale = jnp.broadcast_to(scales[...], (128, tokens)).T
    scale = jnp.concatenate([scale] * (half // 128), axis=1)
    expert_row, slot_row = experts[...].astype(jnp.float32), slots[...].astype(jnp.float32)
    row = lax.broadcasted_iota(jnp.int32, (TAIL, tokens), 0)
    ids = jnp.where(row == 0, expert_row, jnp.where(row == 1, slot_row, 0.0)).astype(jnp.bfloat16)
    for mask in order:
        large[mask].wait()
        halves = []
        for side in range(2):
            begin = pl.multiple_of((core ^ side) * half, half)
            block = cot[mask, :, pl.ds(begin, half)].astype(jnp.float32)
            halves.append((scale * block).astype(jnp.bfloat16))
        routed = jnp.concatenate(halves, axis=1)
        if mask:
            out = blocks[mask - 1]
            out[:tokens, :] = routed
            out[tokens:, :] = jnp.concatenate([ids] * (part // tokens), axis=1)
        else:
            z = lax.axis_index("expert")
            for shift, out in enumerate(packed):
                expert = lax.rem(z + shift, owners)
                out[...] = packed_rows(routed, expert_row, slot_row, expert, capacity)


def pack_kernel(owners, capacity, n_blocks, *refs):
    z = lax.axis_index("expert")
    blocks, outs = refs[:n_blocks], refs[-owners:]
    tokens = blocks[0].shape[0] - TAIL
    for at, block in enumerate(blocks):
        ids = block[tokens:, :tokens].astype(jnp.float32)
        rows = block[:tokens, :]
        for shift, out in enumerate(outs):
            expert = lax.rem(z + shift, owners)
            out[at * capacity : (at + 1) * capacity, :] = packed_rows(rows, ids[0:1], ids[1:2], expert, capacity)


def product_kernel(owners, capacity, columns, first, plan, n_early, *refs):
    me = lax.axis_index("expert")
    used = 1 + max(max(max(parts), max(place for place, _, _ in packed)) for parts, packed in plan)
    early, out = refs[used : used + n_early], refs[-1]
    rows = [
        jnp.concatenate([refs[place][at * capacity : (at + 1) * capacity, columns] for place, at, _ in packed])
        for _, packed in plan
    ]
    wide = min(out.shape[1], *(refs[place].shape[1] for parts, _ in plan for place in parts))
    for column in range(first, first + out.shape[1], wide):
        total = None
        for left, (parts, packed) in zip(rows, plan):
            size = refs[parts[0]].shape[1]
            part = refs[parts[column // size]]
            inside = slice(column % size, column % size + wide)
            begins = [lax.rem(me + owners - shift, owners) * capacity for _, _, shift in packed]
            right = [part[pl.ds(pl.multiple_of(begin, capacity), capacity), inside] for begin in begins]
            term = lax.dot_general(left, jnp.concatenate(right), ROWS_FIRST, preferred_element_type=jnp.float32)
            total = term if total is None else total + term
        for ref in early:
            total = total + ref[:, column : column + wide]
        out[:, column - first : column - first + wide] = total


def new_moments(grad, first, second):
    return 0.9 * first + 0.1 * grad, 0.999 * second + 0.001 * grad * grad


def update_kernel(begin, mine_ref, other_ref, weight_ref, first_ref, second_ref, *refs):
    earlier, (grad_ref, update_ref, sums) = refs[:-3], refs[-3:]
    columns = slice(begin, begin + other_ref.shape[1])
    grad = mine_ref[:, columns] + other_ref[...]
    grad_ref[...] = grad
    weight = weight_ref[0, :, columns]
    first, second = new_moments(grad, first_ref[0, :, columns], second_ref[0, :, columns])
    first, second = first * (1.0 / (1.0 - 0.9**10)), second * (1.0 / (1.0 - 0.999**10))
    root = second * lax.rsqrt(second)
    update = first * pl.reciprocal(root + 1e-06) + 0.01 * weight
    update_ref[...] = update
    row = lax.broadcasted_iota(jnp.int32, sums.shape, 0)
    total = jnp.where(row == 0, jnp.sum(weight * weight), jnp.sum(update * update))
    for ref in earlier:
        total = total + ref[...]
    sums[...] = total


def moment_kernel(left_ref, right_ref, first_ref, second_ref, new_first, new_second):
    begin = 0
    for grad_ref in (left_ref, right_ref):
        columns = slice(begin, begin + grad_ref.shape[1])
        first, second = new_moments(grad_ref[...], first_ref[0, :, columns], second_ref[0, :, columns])
        new_first[0, :, columns], new_second[0, :, columns] = first, second
        begin += grad_ref.shape[1]


def weight_kernel(n_sums, *refs):
    sums, (weight_ref, left_ref, right_ref, out_ref, new_weight, sems) = refs[:n_sums], refs[n_sums:]
    total = sums[0][...]
    for other in sums[1:]:
        total = total + other[...]
    norm = jnp.sqrt(total)
    scale = 0.1 * (norm[0:1, 0:1] / (norm[1:2, 0:1] + 1e-06))
    n = sems.shape[0]
    rows = left_ref.shape[0] // n
    copies = []
    for at in range(n):
        span = pl.ds(at * rows, rows)
        update = jnp.concatenate([left_ref[span, :], right_ref[span, :]], axis=1)
        new_weight[0, span, :] = weight_ref[0, span, :] - scale * update
        copies.append(pltpu.make_async_copy(new_weight.at[:, span], out_ref.at[:, span], sems.at[at]))
        copies[-1].start()
    for copy in copies:
        copy.wait()


def call(kernel, out_shape, *args, spaces=VMEM, out_spaces=VMEM, scratch=(), flops=0, name=None):
    nbytes = sum(a.size * a.dtype.itemsize for a in jax.tree.leaves((args, out_shape)))
    return pl.pallas_call(
        kernel,
        out_shape=out_shape,
        in_specs=spaces if isinstance(spaces, list) else [spaces] * len(args),
        out_specs=jax.tree.map(lambda _: out_spaces, out_shape),
        scratch_shapes=scratch,
        compiler_params=pltpu.CompilerParams(vmem_limit_bytes=40 * 2**20),
        cost_estimate=pl.CostEstimate(flops=flops, bytes_accessed=nbytes, transcendentals=0),
        name=name,
    )(*args)


def tick(*arrays, flops):
    def kernel(*refs):
        refs[-1][...] = jnp.zeros(refs[-1].shape, jnp.float32)

    return call(kernel, jax.ShapeDtypeStruct((8, 128), jnp.float32), *arrays, spaces=ANY, flops=flops, name="tick")


def after(arrays, *earlier):
    return lax.optimization_barrier((arrays, earlier))[0]


def by_permutes(
    cotangent,
    route_weight,
    expert_ids,
    slot_ids,
    hidden_saved,
    down_weight,
    first_moment,
    second_moment,
):
    n_dp, owners = lax.axis_size("dp"), lax.axis_size("expert")
    n_chips = n_dp // 2
    tokens, width = cotangent.shape
    capacity, ff = hidden_saved.shape[3:]
    part = width // n_chips
    half = part // 2
    bf16, f32 = jnp.bfloat16, jnp.float32
    hidden = hidden_saved.reshape(owners * capacity, ff)

    def across(array, mask):
        return lax.ppermute(array, "dp", [(d, d ^ mask) for d in range(n_dp)])

    def along(array, shift):
        return lax.ppermute(array, "expert", [(d, (d + shift) % owners) for d in range(owners)])

    def pack(*blocks, waits=()):
        size = len(blocks) * capacity
        return call(
            functools.partial(pack_kernel, owners, capacity, len(blocks)),
            [jax.ShapeDtypeStruct((size, part), bf16)] * owners,
            *blocks,
            *waits,
            spaces=[VMEM] * len(blocks) + [ANY] * len(waits),
            flops=4 * 2 * size * owners * tokens * part,
            name="pack",
        )

    def multiply(columns, groups, *early, span=slice(0, ff), waits=()):
        arrays, plan = [], []

        def place(array):
            if not any(array is other for other in arrays):
                arrays.append(array)
            return [array is other for other in arrays].index(True)

        for parts, packed in groups:
            plan.append(([place(p) for p in parts], [(place(p), at, shift) for p, at, shift in packed]))
        n = columns.stop - columns.start
        return call(
            functools.partial(product_kernel, owners, capacity, columns, span.start, plan, len(early)),
            jax.ShapeDtypeStruct((n, span.stop - span.start), f32),
            *arrays,
            *early,
            *waits,
            spaces=[VMEM] * (len(arrays) + len(early)) + [ANY] * len(waits),
            flops=2 * sum(len(packed) for _, packed in plan) * capacity * n * (span.stop - span.start),
            name="product",
        )

    packed, block = jax.ShapeDtypeStruct((capacity, part), bf16), jax.ShapeDtypeStruct((tokens + TAIL, part), bf16)
    operands = cotangent, *[ids.reshape(1, tokens) for ids in (route_weight, expert_ids, slot_ids)]
    cut = call(
        functools.partial(cut_kernel, n_chips, owners, capacity),
        [packed] * owners + [block] * (n_chips - 1),
        *[pltpu.with_memory_space_constraint(array, pltpu.HBM) for array in operands],
        spaces=HBM,
        scratch=[
            pltpu.VMEM((n_chips, tokens, part), bf16),
            pltpu.VMEM((1, tokens), f32),
            pltpu.VMEM((1, tokens), jnp.int32),
            pltpu.VMEM((1, tokens), jnp.int32),
            pltpu.SemaphoreType.DMA((3 + n_chips,)),
        ],
        name="cut",
    )
    near, (to_x, to_y, to_xy) = cut[:owners], cut[owners:]
    from_x, from_y = across(to_x, 2), across(to_y, 4)
    near = [near[0]] + [along(near[shift], shift) for shift in range(1, owners)]
    seen = tick(near[2], flops=2 * UNIT)
    mid = pack(from_x, waits=[seen])
    mid = [mid[0]] + [along(mid[shift], shift) for shift in range(1, owners)]
    late = tick(near[1], near[3], flops=2 * UNIT)
    from_xy = across(after(to_xy, from_x, from_y, seen), 6)
    far = pack(from_y, from_xy, waits=[late])
    far = [far[0]] + [along(far[shift], shift) for shift in range(1, owners)]
    sent = after(hidden, from_x, from_y, near[2], late)
    by_x, by_y = across(sent, 2), across(sent, 4)
    by_xy = across(by_x[:, : ff // 2], 4), across(by_y[:, ff // 2 :], 2)

    def terms(packed, at, *shifts):
        return [(packed[shift], at, shift) for shift in shifts]

    keep, give = slice(0, half), slice(half, part)
    spans = slice(0, ff // 2), slice(ff // 2, ff)
    state_in = down_weight, first_moment, second_moment
    seen = tick(*mid[1:], flops=20 * UNIT)
    groups = [((hidden,), terms(near, 0, 0, 1, 2, 3)), ((by_x,), terms(mid, 0, 0, 1, 2, 3))]
    total = {side: multiply(side, groups, waits=[seen]) for side in (give, keep)}
    seen = tick(far[1], far[3], *total.values(), flops=5 * UNIT)
    groups = [((by_y,), terms(far, 0, 0, 1, 3)), (by_xy, terms(far, 1, 0, 1, 3))]
    total = {side: multiply(side, groups, early, waits=[seen, *state_in]) for side, early in total.items()}
    seen = tick(far[2], *total.values(), flops=5 * UNIT)
    groups = [((by_y,), terms(far, 0, 2)), (by_xy, terms(far, 1, 2))]
    given = [multiply(give, groups, total[give], span=span, waits=[seen]) for span in spans]
    other = [across(part, 1) for part in given]
    kept = multiply(keep, groups, after(total[keep], *given))

    state = jax.ShapeDtypeStruct((1, half, ff), f32)
    grads, updates, sums = [], [], []
    for span, part in zip(spans, other):
        piece = jax.ShapeDtypeStruct(part.shape, f32)
        grad, update, total = call(
            functools.partial(update_kernel, span.start),
            [piece, piece, jax.ShapeDtypeStruct((8, 128), f32)],
            kept,
            part,
            *state_in,
            *sums,
            name="update",
        )
        grads, updates, sums = [*grads, grad], [*updates, update], [total]
    sums = sums[0] + across(sums[0], 1)
    parts = [sums] + [across(sums, mask) for mask in (2, 4, 6)]
    new_first, new_second = call(
        moment_kernel, [state, state], *after(tuple(grads), sums), first_moment, second_moment, name="moment"
    )
    new_weight = call(
        functools.partial(weight_kernel, len(parts)),
        state,
        *parts,
        down_weight,
        *updates,
        out_spaces=HBM,
        scratch=[pltpu.VMEM((1, half, ff), f32), pltpu.SemaphoreType.DMA((4,))],
        name="weight",
    )
    return new_weight, new_first, new_second


def solution(mesh):
    placed = (
        P(("dp", "expert"), None),
        P(("dp", "expert")),
        P(("dp", "expert")),
        P(("dp", "expert")),
        P("dp", "expert", None, None, None),
        P("expert", "dp", None),
        P("expert", "dp", None),
        P("expert", "dp", None),
    )
    return jax.shard_map(
        by_permutes if (mesh.shape["dp"], mesh.shape["expert"]) == (8, 4) else on_device,
        mesh=mesh,
        in_specs=placed,
        out_specs=(P("expert", "dp", None), P("expert", "dp", None), P("expert", "dp", None)),
        check_vma=False,
    )
```

```python
import functools

import jax
import jax.numpy as jnp
from jax import lax
from jax.experimental import pallas as pl
from jax.experimental.pallas import tpu as pltpu
from jax.sharding import PartitionSpec as P

VMEM = pl.BlockSpec(memory_space=pltpu.VMEM)
HBM = pl.BlockSpec(memory_space=pltpu.HBM)
ANY = pl.BlockSpec(memory_space=pl.ANY)
TAIL = 16
ROWS_FIRST = (((0,), (0,)), ((), ()))
UNIT = 10**9


def on_device(
    cotangent,
    route_weight,
    expert_ids,
    slot_ids,
    hidden_saved,
    down_weight,
    first_moment,
    second_moment,
):
    tok_rows, width = cotangent.shape
    owners = lax.axis_size("expert")
    hidden_rows = hidden_saved.reshape(-1, hidden_saved.shape[-1])
    capacity = hidden_rows.shape[0] // owners
    weight = down_weight[0]
    routed = (route_weight[:, None] * cotangent.astype(jnp.float32)).astype(jnp.bfloat16)
    target = expert_ids * capacity + slot_ids
    outgoing = jnp.zeros((owners * capacity, width), jnp.bfloat16).at[target].set(routed)
    arrived = lax.all_to_all(
        outgoing.reshape(owners, capacity, width), "expert", split_axis=0, concat_axis=0, tiled=True
    )
    arrived = arrived.reshape(owners * capacity, width)
    whole_term = lax.dot_general(
        arrived, hidden_rows, (((0,), (0,)), ((), ())), preferred_element_type=jnp.float32
    )
    grad = lax.psum_scatter(whole_term, "dp", scatter_dimension=0, tiled=True)
    new_first = 0.9 * first_moment[0] + 0.1 * grad
    new_second = 0.999 * second_moment[0] + 0.001 * grad * grad
    update = (
        new_first / (1.0 - 0.9**10) / (jnp.sqrt(new_second / (1.0 - 0.999**10)) + 1e-06)
        + 0.01 * weight
    )
    weight_sq, update_sq = lax.psum((jnp.sum(weight * weight), jnp.sum(update * update)), "dp")
    ratio = jnp.sqrt(weight_sq) / (jnp.sqrt(update_sq) + 1e-06)
    new_weight = weight - 0.1 * ratio * update
    return (new_weight[None], new_first[None], new_second[None])


def packed_rows(rows, expert_row, slot_row, expert, capacity):
    slot = lax.broadcasted_iota(jnp.int32, (capacity, rows.shape[0]), 0).astype(jnp.float32)
    place = (expert_row - expert.astype(jnp.float32)) * capacity + slot_row
    hot = jnp.where(slot == place, 1.0, 0.0).astype(jnp.bfloat16)
    return jnp.dot(hot, rows, preferred_element_type=jnp.float32).astype(jnp.bfloat16)


def cut_kernel(n_chips, owners, capacity, cot_ref, scale_ref, expert_ref, slot_ref, *refs):
    packed, blocks = refs[:owners], refs[owners : owners + n_chips - 1]
    cot, scales, experts, slots, sems = refs[owners + n_chips - 1 :]
    tokens, width = cot_ref.shape
    part = width // n_chips
    half = part // 2
    me = lax.axis_index("dp")
    chip, core = me // 2, lax.rem(me, 2)
    small = [
        pltpu.make_async_copy(src, dst, sems.at[at])
        for at, (src, dst) in enumerate([(scale_ref, scales), (expert_ref, experts), (slot_ref, slots)])
    ]
    large = []
    for mask in range(n_chips):
        columns = pl.ds(pl.multiple_of((chip ^ mask) * part, part), part)
        large.append(pltpu.make_async_copy(cot_ref.at[:, columns], cot.at[mask], sems.at[3 + mask]))
    order = (*range(1, n_chips), 0)
    for copy in small + [large[mask] for mask in order]:
        copy.start()
    for copy in small:
        copy.wait()
    scale = jnp.broadcast_to(scales[...], (128, tokens)).T
    scale = jnp.concatenate([scale] * (half // 128), axis=1)
    expert_row, slot_row = experts[...].astype(jnp.float32), slots[...].astype(jnp.float32)
    row = lax.broadcasted_iota(jnp.int32, (TAIL, tokens), 0)
    ids = jnp.where(row == 0, expert_row, jnp.where(row == 1, slot_row, 0.0)).astype(jnp.bfloat16)
    for mask in order:
        large[mask].wait()
        halves = []
        for side in range(2):
            begin = pl.multiple_of((core ^ side) * half, half)
            block = cot[mask, :, pl.ds(begin, half)].astype(jnp.float32)
            halves.append((scale * block).astype(jnp.bfloat16))
        routed = jnp.concatenate(halves, axis=1)
        if mask:
            out = blocks[mask - 1]
            out[:tokens, :] = routed
            out[tokens:, :] = jnp.concatenate([ids] * (part // tokens), axis=1)
        else:
            z = lax.axis_index("expert")
            for shift, out in enumerate(packed):
                expert = lax.rem(z + shift, owners)
                out[...] = packed_rows(routed, expert_row, slot_row, expert, capacity)


def pack_kernel(owners, capacity, n_blocks, n_outs, *refs):
    z = lax.axis_index("expert")
    blocks, outs = refs[:n_blocks], refs[-n_outs:]
    tokens = blocks[0].shape[0] - TAIL
    for at, block in enumerate(blocks):
        ids = block[tokens:, :tokens].astype(jnp.float32)
        rows = block[:tokens, :]
        span = slice(at * capacity, (at + 1) * capacity)
        for shift in range(owners):
            packed = packed_rows(rows, ids[0:1], ids[1:2], lax.rem(z + shift, owners), capacity)
            for at_out, out in enumerate(outs[shift:] if shift == owners - 1 else outs[shift : shift + 1]):
                wide = out.shape[1]
                out[span, :] = packed[:, at_out * wide : (at_out + 1) * wide]


def pick_kernel(owners, capacity, *refs):
    parts, out = refs[:-1], refs[-1]
    begin = pl.multiple_of(lax.rem(lax.axis_index("expert") + 1, owners) * capacity, capacity)
    out[...] = jnp.concatenate([part[pl.ds(begin, capacity), :] for part in parts], axis=1)


def product_kernel(owners, capacity, columns, first, plan, n_early, *refs):
    me = lax.axis_index("expert")
    used = 1 + max(max(max(parts), max(place for place, _, _ in packed)) for parts, packed in plan)
    early, out = refs[used : used + n_early], refs[-1]
    rows = [
        jnp.concatenate([refs[place][at * capacity : (at + 1) * capacity, columns] for place, at, _ in packed])
        for _, packed in plan
    ]
    wide = min(out.shape[1], *(refs[place].shape[1] for parts, _ in plan for place in parts))
    for column in range(first, first + out.shape[1], wide):
        total = None
        for left, (parts, packed) in zip(rows, plan):
            size = refs[parts[0]].shape[1]
            part = refs[parts[column // size]]
            inside = slice(column % size, column % size + wide)
            begins = [0 if shift is None else lax.rem(me + owners - shift, owners) * capacity for _, _, shift in packed]
            right = [part[pl.ds(pl.multiple_of(begin, capacity), capacity), inside] for begin in begins]
            term = lax.dot_general(left, jnp.concatenate(right), ROWS_FIRST, preferred_element_type=jnp.float32)
            total = term if total is None else total + term
        for ref in early:
            total = total + ref[:, column : column + wide]
        out[:, column - first : column - first + wide] = total


def new_moments(grad, first, second):
    return 0.9 * first + 0.1 * grad, 0.999 * second + 0.001 * grad * grad


def update_kernel(begin, mine_ref, other_ref, weight_ref, first_ref, second_ref, *refs):
    earlier, (grad_ref, update_ref, sums) = refs[:-3], refs[-3:]
    columns = slice(begin, begin + other_ref.shape[1])
    grad = mine_ref[:, columns] + other_ref[...]
    grad_ref[...] = grad
    weight = weight_ref[0, :, columns]
    first, second = new_moments(grad, first_ref[0, :, columns], second_ref[0, :, columns])
    first, second = first * (1.0 / (1.0 - 0.9**10)), second * (1.0 / (1.0 - 0.999**10))
    root = second * lax.rsqrt(second)
    update = first * pl.reciprocal(root + 1e-06) + 0.01 * weight
    update_ref[...] = update
    row = lax.broadcasted_iota(jnp.int32, sums.shape, 0)
    total = jnp.where(row == 0, jnp.sum(weight * weight), jnp.sum(update * update))
    for ref in earlier:
        total = total + ref[...]
    sums[...] = total


def moment_kernel(left_ref, right_ref, first_ref, second_ref, new_first, new_second):
    begin = 0
    for grad_ref in (left_ref, right_ref):
        columns = slice(begin, begin + grad_ref.shape[1])
        first, second = new_moments(grad_ref[...], first_ref[0, :, columns], second_ref[0, :, columns])
        new_first[0, :, columns], new_second[0, :, columns] = first, second
        begin += grad_ref.shape[1]


def weight_kernel(n_sums, *refs):
    sums, (weight_ref, left_ref, right_ref, out_ref, new_weight, sems) = refs[:n_sums], refs[n_sums:]
    total = sums[0][...]
    for other in sums[1:]:
        total = total + other[...]
    norm = jnp.sqrt(total)
    scale = 0.1 * (norm[0:1, 0:1] / (norm[1:2, 0:1] + 1e-06))
    n = sems.shape[0]
    rows = left_ref.shape[0] // n
    copies = []
    for at in range(n):
        span = pl.ds(at * rows, rows)
        update = jnp.concatenate([left_ref[span, :], right_ref[span, :]], axis=1)
        new_weight[0, span, :] = weight_ref[0, span, :] - scale * update
        copies.append(pltpu.make_async_copy(new_weight.at[:, span], out_ref.at[:, span], sems.at[at]))
        copies[-1].start()
    for copy in copies:
        copy.wait()


def call(kernel, out_shape, *args, spaces=VMEM, out_spaces=VMEM, scratch=(), flops=0, name=None):
    nbytes = sum(a.size * a.dtype.itemsize for a in jax.tree.leaves((args, out_shape)))
    return pl.pallas_call(
        kernel,
        out_shape=out_shape,
        in_specs=spaces if isinstance(spaces, list) else [spaces] * len(args),
        out_specs=jax.tree.map(lambda _: out_spaces, out_shape),
        scratch_shapes=scratch,
        compiler_params=pltpu.CompilerParams(vmem_limit_bytes=40 * 2**20),
        cost_estimate=pl.CostEstimate(flops=flops, bytes_accessed=nbytes, transcendentals=0),
        name=name,
    )(*args)


def tick(*arrays, flops):
    def kernel(*refs):
        refs[-1][...] = jnp.zeros(refs[-1].shape, jnp.float32)

    return call(kernel, jax.ShapeDtypeStruct((8, 128), jnp.float32), *arrays, spaces=ANY, flops=flops, name="tick")


def after(arrays, *earlier):
    return lax.optimization_barrier((arrays, earlier))[0]


def by_permutes(
    cotangent,
    route_weight,
    expert_ids,
    slot_ids,
    hidden_saved,
    down_weight,
    first_moment,
    second_moment,
):
    n_dp, owners = lax.axis_size("dp"), lax.axis_size("expert")
    n_chips = n_dp // 2
    tokens, width = cotangent.shape
    capacity, ff = hidden_saved.shape[3:]
    part = width // n_chips
    half = part // 2
    bf16, f32 = jnp.bfloat16, jnp.float32
    hidden = hidden_saved.reshape(owners * capacity, ff)

    def across(array, mask):
        return lax.ppermute(array, "dp", [(d, d ^ mask) for d in range(n_dp)])

    def along(array, shift):
        return lax.ppermute(array, "expert", [(d, (d + shift) % owners) for d in range(owners)])

    def pack(*blocks, halves=1, waits=()):
        size = len(blocks) * capacity
        widths = [part] * (owners - 1) + [part // halves] * halves
        return call(
            functools.partial(pack_kernel, owners, capacity, len(blocks), len(widths)),
            [jax.ShapeDtypeStruct((size, wide), bf16) for wide in widths],
            *blocks,
            *waits,
            spaces=[VMEM] * len(blocks) + [ANY] * len(waits),
            flops=4 * 2 * size * owners * tokens * part,
            name="pack",
        )

    def pick(*parts):
        shape = jax.ShapeDtypeStruct((capacity, ff), bf16)
        return across(call(functools.partial(pick_kernel, owners, capacity), shape, *parts, name="pick"), 1)

    def to_sibling(array, shift):
        pairs = []
        for d in range(n_dp):
            for e in range(owners):
                pairs.append((d * owners + e, (d ^ 1) * owners + (e + shift) % owners))
        return lax.ppermute(array, ("dp", "expert"), pairs)

    def multiply(columns, groups, *early, span=slice(0, ff), waits=()):
        arrays, plan = [], []

        def place(array):
            if not any(array is other for other in arrays):
                arrays.append(array)
            return [array is other for other in arrays].index(True)

        for parts, packed in groups:
            plan.append(([place(p) for p in parts], [(place(p), at, shift) for p, at, shift in packed]))
        n = columns.stop - columns.start
        return call(
            functools.partial(product_kernel, owners, capacity, columns, span.start, plan, len(early)),
            jax.ShapeDtypeStruct((n, span.stop - span.start), f32),
            *arrays,
            *early,
            *waits,
            spaces=[VMEM] * (len(arrays) + len(early)) + [ANY] * len(waits),
            flops=2 * sum(len(packed) for _, packed in plan) * capacity * n * (span.stop - span.start),
            name="product",
        )

    packed, block = jax.ShapeDtypeStruct((capacity, part), bf16), jax.ShapeDtypeStruct((tokens + TAIL, part), bf16)
    operands = cotangent, *[ids.reshape(1, tokens) for ids in (route_weight, expert_ids, slot_ids)]
    cut = call(
        functools.partial(cut_kernel, n_chips, owners, capacity),
        [packed] * owners + [block] * (n_chips - 1),
        *[pltpu.with_memory_space_constraint(array, pltpu.HBM) for array in operands],
        spaces=HBM,
        scratch=[
            pltpu.VMEM((n_chips, tokens, part), bf16),
            pltpu.VMEM((1, tokens), f32),
            pltpu.VMEM((1, tokens), jnp.int32),
            pltpu.VMEM((1, tokens), jnp.int32),
            pltpu.SemaphoreType.DMA((3 + n_chips,)),
        ],
        name="cut",
    )
    near, (to_x, to_y, to_xy) = cut[:owners], cut[owners:]
    from_x, from_y = across(to_x, 2), across(to_y, 4)
    near = [near[0]] + [along(near[shift], shift) for shift in range(1, owners)]
    seen = tick(near[2], flops=2 * UNIT)
    mid = pack(from_x, waits=[seen])
    mid = [mid[0]] + [along(mid[shift], shift) for shift in range(1, owners)]
    late = tick(near[1], near[3], flops=2 * UNIT)
    from_xy = across(after(to_xy, from_x, from_y, seen), 6)
    far = pack(from_y, from_xy, halves=2, waits=[late])
    far = [far[0]] + [along(far[shift], shift) for shift in range(1, owners)] + [far[owners]]
    sent = after(hidden, from_x, from_y, near[2], late)
    by_x, by_y = across(sent, 2), across(sent, 4)
    by_xy = across(by_x[:, : ff // 2], 4), across(by_y[:, ff // 2 :], 2)

    def terms(packed, at, *shifts):
        return [(packed[shift], at, shift) for shift in shifts]

    keep, give = slice(0, half), slice(half, part)
    spans = slice(0, ff // 2), slice(ff // 2, ff)
    state_in = down_weight, first_moment, second_moment
    seen = tick(*mid[1:], flops=20 * UNIT)
    groups = [((hidden,), terms(near, 0, 0, 1, 2, 3)), ((by_x,), terms(mid, 0, 0, 1, 2, 3))]
    total = {side: multiply(side, groups, waits=[seen, by_y]) for side in (give, keep)}
    far[4] = to_sibling(after(far[4], far[1], by_x, by_y, *total.values()), 3)
    seen = tick(far[1], far[2], *total.values(), flops=5 * UNIT)
    groups = [((by_y,), terms(far, 0, 0, 1, 2)), (by_xy, terms(far, 1, 0, 1, 2))]
    given = [multiply(give, groups, total[give], span=span, waits=[seen, *state_in]) for span in spans]
    other = [across(part, 1) for part in given]
    picked = pick(after(by_y, given[0])), pick(*after(by_xy, given[0]))
    kept = multiply(keep, groups, total[keep], waits=[seen])
    seen = tick(far[3], far[4], kept, flops=5 * UNIT)
    groups = [((by_y,), [(far[3], 0, 3)]), (by_xy, [(far[3], 1, 3)])]
    groups += [((picked[0],), [(far[4], 0, None)]), ((picked[1],), [(far[4], 1, None)])]
    kept = multiply(keep, groups, kept, waits=[seen])

    state = jax.ShapeDtypeStruct((1, half, ff), f32)
    grads, updates, sums = [], [], []
    for span, part in zip(spans, other):
        piece = jax.ShapeDtypeStruct(part.shape, f32)
        grad, update, total = call(
            functools.partial(update_kernel, span.start),
            [piece, piece, jax.ShapeDtypeStruct((8, 128), f32)],
            kept,
            part,
            *state_in,
            *sums,
            name="update",
        )
        grads, updates, sums = [*grads, grad], [*updates, update], [total]
    sums = sums[0] + across(sums[0], 1)
    parts = [sums] + [across(sums, mask) for mask in (2, 4, 6)]
    new_first, new_second = call(
        moment_kernel, [state, state], *after(tuple(grads), sums), first_moment, second_moment, name="moment"
    )
    new_weight = call(
        functools.partial(weight_kernel, len(parts)),
        state,
        *parts,
        down_weight,
        *updates,
        out_spaces=HBM,
        scratch=[pltpu.VMEM((1, half, ff), f32), pltpu.SemaphoreType.DMA((4,))],
        name="weight",
    )
    return new_weight, new_first, new_second


def solution(mesh):
    placed = (
        P(("dp", "expert"), None),
        P(("dp", "expert")),
        P(("dp", "expert")),
        P(("dp", "expert")),
        P("dp", "expert", None, None, None),
        P("expert", "dp", None),
        P("expert", "dp", None),
        P("expert", "dp", None),
    )
    return jax.shard_map(
        by_permutes if (mesh.shape["dp"], mesh.shape["expert"]) == (8, 4) else on_device,
        mesh=mesh,
        in_specs=placed,
        out_specs=(P("expert", "dp", None), P("expert", "dp", None), P("expert", "dp", None)),
        check_vma=False,
    )
```

```python
import functools

import jax
import jax.numpy as jnp
from jax import lax
from jax.experimental import pallas as pl
from jax.experimental.pallas import tpu as pltpu
from jax.sharding import PartitionSpec as P

VMEM = pl.BlockSpec(memory_space=pltpu.VMEM)
HBM = pl.BlockSpec(memory_space=pltpu.HBM)
ANY = pl.BlockSpec(memory_space=pl.ANY)
TAIL = 16
ROWS_FIRST = (((0,), (0,)), ((), ()))
UNIT = 10**9


def on_device(
    cotangent,
    route_weight,
    expert_ids,
    slot_ids,
    hidden_saved,
    down_weight,
    first_moment,
    second_moment,
):
    tok_rows, width = cotangent.shape
    owners = lax.axis_size("expert")
    hidden_rows = hidden_saved.reshape(-1, hidden_saved.shape[-1])
    capacity = hidden_rows.shape[0] // owners
    weight = down_weight[0]
    routed = (route_weight[:, None] * cotangent.astype(jnp.float32)).astype(jnp.bfloat16)
    target = expert_ids * capacity + slot_ids
    outgoing = jnp.zeros((owners * capacity, width), jnp.bfloat16).at[target].set(routed)
    arrived = lax.all_to_all(
        outgoing.reshape(owners, capacity, width), "expert", split_axis=0, concat_axis=0, tiled=True
    )
    arrived = arrived.reshape(owners * capacity, width)
    whole_term = lax.dot_general(
        arrived, hidden_rows, (((0,), (0,)), ((), ())), preferred_element_type=jnp.float32
    )
    grad = lax.psum_scatter(whole_term, "dp", scatter_dimension=0, tiled=True)
    new_first = 0.9 * first_moment[0] + 0.1 * grad
    new_second = 0.999 * second_moment[0] + 0.001 * grad * grad
    update = (
        new_first / (1.0 - 0.9**10) / (jnp.sqrt(new_second / (1.0 - 0.999**10)) + 1e-06)
        + 0.01 * weight
    )
    weight_sq, update_sq = lax.psum((jnp.sum(weight * weight), jnp.sum(update * update)), "dp")
    ratio = jnp.sqrt(weight_sq) / (jnp.sqrt(update_sq) + 1e-06)
    new_weight = weight - 0.1 * ratio * update
    return (new_weight[None], new_first[None], new_second[None])


def packed_rows(rows, expert_row, slot_row, expert, capacity):
    slot = lax.broadcasted_iota(jnp.int32, (capacity, rows.shape[0]), 0).astype(jnp.float32)
    place = (expert_row - expert.astype(jnp.float32)) * capacity + slot_row
    hot = jnp.where(slot == place, 1.0, 0.0).astype(jnp.bfloat16)
    return jnp.dot(hot, rows, preferred_element_type=jnp.float32).astype(jnp.bfloat16)


def cut_kernel(n_chips, owners, capacity, cot_ref, scale_ref, expert_ref, slot_ref, *refs):
    packed, blocks = refs[:owners], refs[owners : owners + n_chips - 1]
    cot, scales, experts, slots, sems = refs[owners + n_chips - 1 :]
    tokens, width = cot_ref.shape
    part = width // n_chips
    half = part // 2
    me = lax.axis_index("dp")
    chip, core = me // 2, lax.rem(me, 2)
    small = [
        pltpu.make_async_copy(src, dst, sems.at[at])
        for at, (src, dst) in enumerate([(scale_ref, scales), (expert_ref, experts), (slot_ref, slots)])
    ]
    large = []
    for mask in range(n_chips):
        columns = pl.ds(pl.multiple_of((chip ^ mask) * part, part), part)
        large.append(pltpu.make_async_copy(cot_ref.at[:, columns], cot.at[mask], sems.at[3 + mask]))
    order = (*range(1, n_chips), 0)
    for copy in small + [large[mask] for mask in order]:
        copy.start()
    for copy in small:
        copy.wait()
    scale = jnp.broadcast_to(scales[...], (128, tokens)).T
    scale = jnp.concatenate([scale] * (half // 128), axis=1)
    expert_row, slot_row = experts[...].astype(jnp.float32), slots[...].astype(jnp.float32)
    row = lax.broadcasted_iota(jnp.int32, (TAIL, tokens), 0)
    ids = jnp.where(row == 0, expert_row, jnp.where(row == 1, slot_row, 0.0)).astype(jnp.bfloat16)
    for mask in order:
        large[mask].wait()
        halves = []
        for side in range(2):
            begin = pl.multiple_of((core ^ side) * half, half)
            block = cot[mask, :, pl.ds(begin, half)].astype(jnp.float32)
            halves.append((scale * block).astype(jnp.bfloat16))
        routed = jnp.concatenate(halves, axis=1)
        if mask:
            out = blocks[mask - 1]
            out[:tokens, :] = routed
            out[tokens:, :] = jnp.concatenate([ids] * (part // tokens), axis=1)
        else:
            z = lax.axis_index("expert")
            for shift, out in enumerate(packed):
                expert = lax.rem(z + shift, owners)
                out[...] = packed_rows(routed, expert_row, slot_row, expert, capacity)


def pack_kernel(owners, capacity, n_blocks, *refs):
    z = lax.axis_index("expert")
    blocks, outs = refs[:n_blocks], refs[-owners:]
    tokens = blocks[0].shape[0] - TAIL
    for at, block in enumerate(blocks):
        ids = block[tokens:, :tokens].astype(jnp.float32)
        rows = block[:tokens, :]
        for shift, out in enumerate(outs):
            expert = lax.rem(z + shift, owners)
            out[at * capacity : (at + 1) * capacity, :] = packed_rows(rows, ids[0:1], ids[1:2], expert, capacity)


def product_kernel(owners, capacity, columns, first, plan, n_early, *refs):
    me = lax.axis_index("expert")
    used = 1 + max(max(max(parts), max(place for place, _, _ in packed)) for parts, packed in plan)
    early, out = refs[used : used + n_early], refs[-1]
    rows = [
        jnp.concatenate([refs[place][at * capacity : (at + 1) * capacity, columns] for place, at, _ in packed])
        for _, packed in plan
    ]
    wide = min(out.shape[1], *(refs[place].shape[1] for parts, _ in plan for place in parts))
    for column in range(first, first + out.shape[1], wide):
        total = None
        for left, (parts, packed) in zip(rows, plan):
            size = refs[parts[0]].shape[1]
            part = refs[parts[column // size]]
            inside = slice(column % size, column % size + wide)
            begins = [lax.rem(me + owners - shift, owners) * capacity for _, _, shift in packed]
            right = [part[pl.ds(pl.multiple_of(begin, capacity), capacity), inside] for begin in begins]
            term = lax.dot_general(left, jnp.concatenate(right), ROWS_FIRST, preferred_element_type=jnp.float32)
            total = term if total is None else total + term
        for ref in early:
            total = total + ref[:, column : column + wide]
        out[:, column - first : column - first + wide] = total


def new_moments(grad, first, second):
    return 0.9 * first + 0.1 * grad, 0.999 * second + 0.001 * grad * grad


def update_kernel(begin, mine_ref, other_ref, weight_ref, first_ref, second_ref, *refs):
    earlier, (grad_ref, update_ref, sums) = refs[:-3], refs[-3:]
    columns = slice(begin, begin + other_ref.shape[1])
    grad = mine_ref[:, columns] + other_ref[...]
    grad_ref[...] = grad
    weight = weight_ref[0, :, columns]
    first, second = new_moments(grad, first_ref[0, :, columns], second_ref[0, :, columns])
    first, second = first * (1.0 / (1.0 - 0.9**10)), second * (1.0 / (1.0 - 0.999**10))
    root = second * lax.rsqrt(second)
    update = first * pl.reciprocal(root + 1e-06) + 0.01 * weight
    update_ref[...] = update
    row = lax.broadcasted_iota(jnp.int32, sums.shape, 0)
    total = jnp.where(row == 0, jnp.sum(weight * weight), jnp.sum(update * update))
    for ref in earlier:
        total = total + ref[...]
    sums[...] = total


def moment_kernel(left_ref, right_ref, first_ref, second_ref, new_first, new_second):
    begin = 0
    for grad_ref in (left_ref, right_ref):
        columns = slice(begin, begin + grad_ref.shape[1])
        first, second = new_moments(grad_ref[...], first_ref[0, :, columns], second_ref[0, :, columns])
        new_first[0, :, columns], new_second[0, :, columns] = first, second
        begin += grad_ref.shape[1]


def weight_kernel(n_sums, *refs):
    sums, (weight_ref, left_ref, right_ref, out_ref, new_weight, sems) = refs[:n_sums], refs[n_sums:]
    total = sums[0][...]
    for other in sums[1:]:
        total = total + other[...]
    norm = jnp.sqrt(total)
    scale = 0.1 * (norm[0:1, 0:1] / (norm[1:2, 0:1] + 1e-06))
    n = sems.shape[0]
    rows = left_ref.shape[0] // n
    copies = []
    for at in range(n):
        span = pl.ds(at * rows, rows)
        update = jnp.concatenate([left_ref[span, :], right_ref[span, :]], axis=1)
        new_weight[0, span, :] = weight_ref[0, span, :] - scale * update
        copies.append(pltpu.make_async_copy(new_weight.at[:, span], out_ref.at[:, span], sems.at[at]))
        copies[-1].start()
    for copy in copies:
        copy.wait()


def call(kernel, out_shape, *args, spaces=VMEM, out_spaces=VMEM, scratch=(), flops=0, name=None):
    nbytes = sum(a.size * a.dtype.itemsize for a in jax.tree.leaves((args, out_shape)))
    return pl.pallas_call(
        kernel,
        out_shape=out_shape,
        in_specs=spaces if isinstance(spaces, list) else [spaces] * len(args),
        out_specs=jax.tree.map(lambda _: out_spaces, out_shape),
        scratch_shapes=scratch,
        compiler_params=pltpu.CompilerParams(vmem_limit_bytes=40 * 2**20),
        cost_estimate=pl.CostEstimate(flops=flops, bytes_accessed=nbytes, transcendentals=0),
        name=name,
    )(*args)


def tick(*arrays, flops):
    def kernel(*refs):
        refs[-1][...] = jnp.zeros(refs[-1].shape, jnp.float32)

    return call(kernel, jax.ShapeDtypeStruct((8, 128), jnp.float32), *arrays, spaces=ANY, flops=flops, name="tick")


def after(arrays, *earlier):
    return lax.optimization_barrier((arrays, earlier))[0]


def by_permutes(
    cotangent,
    route_weight,
    expert_ids,
    slot_ids,
    hidden_saved,
    down_weight,
    first_moment,
    second_moment,
):
    n_dp, owners = lax.axis_size("dp"), lax.axis_size("expert")
    n_chips = n_dp // 2
    tokens, width = cotangent.shape
    capacity, ff = hidden_saved.shape[3:]
    part = width // n_chips
    half = part // 2
    bf16, f32 = jnp.bfloat16, jnp.float32
    hidden = hidden_saved.reshape(owners * capacity, ff)

    def across(array, mask):
        return lax.ppermute(array, "dp", [(d, d ^ mask) for d in range(n_dp)])

    def along(array, shift):
        return lax.ppermute(array, "expert", [(d, (d + shift) % owners) for d in range(owners)])

    def pack(*blocks, waits=()):
        size = len(blocks) * capacity
        return call(
            functools.partial(pack_kernel, owners, capacity, len(blocks)),
            [jax.ShapeDtypeStruct((size, part), bf16)] * owners,
            *blocks,
            *waits,
            spaces=[VMEM] * len(blocks) + [ANY] * len(waits),
            flops=4 * 2 * size * owners * tokens * part,
            name="pack",
        )

    def multiply(columns, groups, *early, span=slice(0, ff), waits=()):
        arrays, plan = [], []

        def place(array):
            if not any(array is other for other in arrays):
                arrays.append(array)
            return [array is other for other in arrays].index(True)

        for parts, packed in groups:
            plan.append(([place(p) for p in parts], [(place(p), at, shift) for p, at, shift in packed]))
        n = columns.stop - columns.start
        return call(
            functools.partial(product_kernel, owners, capacity, columns, span.start, plan, len(early)),
            jax.ShapeDtypeStruct((n, span.stop - span.start), f32),
            *arrays,
            *early,
            *waits,
            spaces=[VMEM] * (len(arrays) + len(early)) + [ANY] * len(waits),
            flops=2 * sum(len(packed) for _, packed in plan) * capacity * n * (span.stop - span.start),
            name="product",
        )

    packed, block = jax.ShapeDtypeStruct((capacity, part), bf16), jax.ShapeDtypeStruct((tokens + TAIL, part), bf16)
    operands = cotangent, *[ids.reshape(1, tokens) for ids in (route_weight, expert_ids, slot_ids)]
    cut = call(
        functools.partial(cut_kernel, n_chips, owners, capacity),
        [packed] * owners + [block] * (n_chips - 1),
        *[pltpu.with_memory_space_constraint(array, pltpu.HBM) for array in operands],
        spaces=HBM,
        scratch=[
            pltpu.VMEM((n_chips, tokens, part), bf16),
            pltpu.VMEM((1, tokens), f32),
            pltpu.VMEM((1, tokens), jnp.int32),
            pltpu.VMEM((1, tokens), jnp.int32),
            pltpu.SemaphoreType.DMA((3 + n_chips,)),
        ],
        name="cut",
    )
    near, (to_x, to_y, to_xy) = cut[:owners], cut[owners:]
    from_x, from_y = across(to_x, 2), across(to_y, 4)
    near = [near[0]] + [along(near[shift], shift) for shift in range(1, owners)]
    seen = tick(near[2], flops=2 * UNIT)
    mid = pack(from_x, waits=[seen])
    mid = [mid[0]] + [along(mid[shift], shift) for shift in range(1, owners)]
    late = tick(near[1], near[3], flops=2 * UNIT)
    from_xy = across(after(to_xy, from_x, from_y, seen), 6)
    far = pack(from_y, from_xy, waits=[late])
    far = [far[0]] + [along(far[shift], shift) for shift in range(1, owners)]
    sent = after(hidden, from_x, from_y, near[2], late)
    by_x, by_y = across(sent, 2), across(sent, 4)
    by_xy = across(by_x[:, : ff // 2], 4), across(by_y[:, ff // 2 :], 2)

    def terms(packed, at, *shifts):
        return [(packed[shift], at, shift) for shift in shifts]

    keep, give = slice(0, half), slice(half, part)
    spans = slice(0, ff // 2), slice(ff // 2, ff)
    state_in = down_weight, first_moment, second_moment
    seen = tick(*mid[1:], flops=20 * UNIT)
    groups = [((hidden,), terms(near, 0, 0, 1, 2, 3)), ((by_x,), terms(mid, 0, 0, 1, 2, 3))]
    total = {side: multiply(side, groups, waits=[seen]) for side in (give, keep)}
    seen = tick(far[1], far[3], *total.values(), flops=5 * UNIT)
    groups = [((by_y,), terms(far, 0, 0, 1, 3)), (by_xy, terms(far, 1, 0, 1, 3))]
    middle = groups
    total[give] = multiply(give, groups, total[give], waits=[seen, *state_in])
    seen = tick(far[2], *total.values(), flops=5 * UNIT)
    groups = [((by_y,), terms(far, 0, 2)), (by_xy, terms(far, 1, 2))]
    given = [multiply(give, groups, total[give], span=span, waits=[seen]) for span in spans]
    other = [across(part, 1) for part in given]
    kept = multiply(keep, middle + groups, after(total[keep], *given))

    state = jax.ShapeDtypeStruct((1, half, ff), f32)
    grads, updates, sums = [], [], []
    for span, part in zip(spans, other):
        piece = jax.ShapeDtypeStruct(part.shape, f32)
        grad, update, total = call(
            functools.partial(update_kernel, span.start),
            [piece, piece, jax.ShapeDtypeStruct((8, 128), f32)],
            kept,
            part,
            *state_in,
            *sums,
            name="update",
        )
        grads, updates, sums = [*grads, grad], [*updates, update], [total]
    sums = sums[0] + across(sums[0], 1)
    parts = [sums] + [across(sums, mask) for mask in (2, 4, 6)]
    new_first, new_second = call(
        moment_kernel, [state, state], *after(tuple(grads), sums), first_moment, second_moment, name="moment"
    )
    new_weight = call(
        functools.partial(weight_kernel, len(parts)),
        state,
        *parts,
        down_weight,
        *updates,
        out_spaces=HBM,
        scratch=[pltpu.VMEM((1, half, ff), f32), pltpu.SemaphoreType.DMA((4,))],
        name="weight",
    )
    return new_weight, new_first, new_second


def solution(mesh):
    placed = (
        P(("dp", "expert"), None),
        P(("dp", "expert")),
        P(("dp", "expert")),
        P(("dp", "expert")),
        P("dp", "expert", None, None, None),
        P("expert", "dp", None),
        P("expert", "dp", None),
        P("expert", "dp", None),
    )
    return jax.shard_map(
        by_permutes if (mesh.shape["dp"], mesh.shape["expert"]) == (8, 4) else on_device,
        mesh=mesh,
        in_specs=placed,
        out_specs=(P("expert", "dp", None), P("expert", "dp", None), P("expert", "dp", None)),
        check_vma=False,
    )
```
